512 devices in a mesh: seq: 64 (over z_lo, x, core), head: 8 (over z_hi, y).
Axes of the slice: x: 4, y: 4, z: 16 (z_hi: 2, z_lo: 8; z = z_hi * 8 + z_lo), core: 2. Of those that a mesh axis runs over, the one named last changes fastest.
Arguments:
- query_nope: bfloat16 [8192, 64, 128], P('seq', 'head'), may hold values from -16 to 16
- query_rotary: bfloat16 [8192, 4096], P('seq', 'head'), may hold values from -12 to 12
- latent: bfloat16 [8192, 512], P('seq'), may hold values from -6 to 6
- rotary_keys: bfloat16 [8192, 64], P('seq'), may hold values from -6 to 6
- output_grad: bfloat16 [8192, 64, 512], P('seq', 'head'), may hold values from -0.3125 to 0.3125
- weight_codes: int32 [128, 64, 512], P('seq', 'head'), may hold values from -128 to 127
- weight_scale: float32 [128, 64], P('seq', 'head'), may hold values from 0.0005 to 0.002
- positions: int32 [8192], P('seq'), may hold values from 0 to 1023, as said below
Outputs:
- query_grad: bfloat16 [8192, 64, 128], P('seq', 'head')
- rotary_grad: bfloat16 [8192, 4096], P('seq', 'head')
- latent_grad: float32 [8192, 512], P('seq')
- keys_grad: float32 [8192, 64], P('seq')
- master_grad: float32 [128, 64, 512], P('seq', 'head')
The draws below stay inside these ranges and needn't reach their ends.
Inputs may be any that keep to these rules, and one draw needn't show every extreme that they name: Each device's tokens form two aligned runs of 64 consecutive positions, each starting at a multiple of 64; the two run numbers (start divided by 64) of a device add up to 15; every position of a document occurs exactly once.
All inputs are finite; a program needn't handle non-finite values.
Results may differ from the reference program's by a relative error of at most 0.017.
Values may be sent and summed in bfloat16 or wider, within the bound.
No kernel may reach another device: no remote copies, remote signals or barrier semaphores. Data moves between devices by JAX's collectives and lax.ppermute only.
A program may use at most 64 MiB of HBM per device.

```python
import math
import jax
import jax.numpy as jnp
from jax import lax

DC = 512
DR = 64
DN = 128
TOK_DEV = 128
DOCS = 8
HEADS = 64
RANKS = 8
DOC_LEN = 1024
TOKENS = 8192


def rotary_pair(key, spread, strength):
    key_first, key_second = jax.random.split(key, 2)
    base_keys = jax.random.uniform(key_first, (TOKENS, DR), jnp.float32, -spread, spread)
    base_query = jax.random.uniform(key_second, (TOKENS, HEADS, DR), jnp.float32, -spread, spread)
    token_phase = jnp.arange(TOKENS) % 16
    leader = strength * (token_phase == 1).astype(jnp.float32)[:, None]
    follower = strength * (token_phase == 0).astype(jnp.float32)[:, None]
    aligned = (1.0 - leader) * base_keys
    rotary_keys = (1.0 - follower) * aligned
    lead_query = leader[:, :, None]
    rotary_query = (1.0 - lead_query) * base_query
    return (rotary_keys, rotary_query.reshape(TOKENS, HEADS * DR))


def draw_query_rotary(key, part):
    shared = rotary_pair(key, 1.7, 0.0)
    return shared[1].astype(jnp.bfloat16)


def draw_rotary_keys(key, part):
    shared = rotary_pair(key, 1.7, 0.0)
    return shared[0].astype(jnp.bfloat16)


def draw_positions(key, part):
    key = jax.random.fold_in(key, 11)
    key_first, key_second = jax.random.split(key, 2)
    half_size = TOK_DEV // 2
    low_tracts = jax.vmap(lambda sub_key: jax.random.permutation(sub_key, RANKS))(jax.random.split(key_first, DOCS))
    flipped = jax.random.randint(key_second, (DOCS, RANKS), 0, 2)
    first_half = jnp.where(flipped == 1, 2 * RANKS - 1 - low_tracts, low_tracts)
    second_half = 2 * RANKS - 1 - first_half
    tracts = jnp.stack([first_half, second_half], axis=-1)
    tracts = jnp.transpose(tracts, (1, 0, 2))
    offsets = jnp.arange(half_size, dtype=jnp.int32)
    placed = tracts[..., None] * half_size + offsets
    return placed.reshape(-1).astype(jnp.int32)


def place_ends(entries, stream_key, low, top_value):
    shape = entries.shape
    spot = [jax.random.randint(jax.random.fold_in(stream_key, axis), (), 0, shape[axis]) for axis in range(len(shape))]
    entries = entries.at[tuple(spot)].set(low)
    longest = shape.index(max(shape))
    spot[longest] = (spot[longest] + 1) % shape[longest]
    return entries.at[tuple(spot)].set(top_value)


def raised(values, rng, source, target, parts, factor):
    owner, partner = [(jnp.arange(values.shape[axis_at]) // (values.shape[axis_at] // parts)).reshape([-1 if axis == axis_at else 1 for axis in range(values.ndim)]) for axis_at in (source, target)]
    chosen = jax.random.permutation(rng, parts)[partner]
    strong = (owner == chosen) | (owner == (partner + parts // 2) % parts)
    return jnp.where(strong, factor * values, values)


def block_levels(rng, extent, cuts, least, top_value):
    gain, own = 1.0, jax.random.fold_in(rng, 6)
    for axis_at, blocks in cuts:
        draws = jnp.exp(jax.random.uniform(jax.random.fold_in(own, axis_at), (blocks,), jnp.float32, least / len(cuts), top_value / len(cuts)))
        gain = gain * jnp.repeat(draws, extent[axis_at] // blocks).reshape([-1 if axis == axis_at else 1 for axis in range(len(extent))])
    return gain


def noise(own_key, extent, deviation, reach, shards=(), held_as=jnp.bfloat16):
    level = block_levels(own_key, extent, shards, -0.22, 0.18) if shards else 1.0
    values = jax.random.normal(own_key, extent, jnp.float32) * deviation * level
    return jnp.minimum(jnp.maximum(values, -reach), reach).astype(held_as)


def bell_draw_with(own_key, extent, deviation, reach, cuts, heavy, kind=jnp.bfloat16):
    entries = deviation * jax.random.normal(own_key, extent, jnp.float32)
    if cuts:
        entries = entries * block_levels(own_key, extent, cuts, -0.22, 0.18)
    return jnp.clip(raised(entries, jax.random.fold_in(own_key, 3), *heavy), -reach, reach).astype(kind)


def setup_inputs(seed: int = 0) -> dict:
    key_list = jax.random.split(jax.random.key(seed), 9)
    query_nope = bell_draw_with(key_list[0], (TOKENS, HEADS, DN), 1.0, 16.0, ((0, 64), (1, 8)), (0, 2, 64, 4.0))
    query_rotary = draw_query_rotary(jax.random.fold_in(key_list[8], 71), 0)
    latent = noise(key_list[2], (TOKENS, DC), 1.0, 6.0, ((0, 64),))
    rotary_keys = draw_rotary_keys(jax.random.fold_in(key_list[8], 71), 0)
    output_grad = noise(key_list[4], (TOKENS, HEADS, DC), 0.05, 0.3125, ((0, 64), (1, 8)))
    weight_codes = place_ends(jax.random.randint(key_list[5], (DN, HEADS, DC), -128, 128), jax.random.fold_in(key_list[5], 1), -128, 127).astype(jnp.int32)
    weight_scale = jnp.clip(jnp.exp(math.log(0.002) - 1.3862944 * jax.random.uniform(key_list[6], (DN, HEADS), jnp.float32) ** block_levels(key_list[6], (DN, HEADS), ((0, 64), (1, 8)), -0.2, 0.2)), 0.0005, 0.002)
    positions = draw_positions(jax.random.fold_in(key_list[8], 71), 0)
    return {"query_nope": query_nope, "query_rotary": query_rotary, "latent": latent, "rotary_keys": rotary_keys, "output_grad": output_grad, "weight_codes": weight_codes, "weight_scale": weight_scale, "positions": positions}


MASKED = -1e+30

def dequant(codes, scales):
    four_bit = 16 * jnp.floor_divide(codes, 16) + 8
    two_bit = 64 * jnp.floor_divide(codes, 64) + 32
    levels = (codes + four_bit + two_bit).astype(jnp.float32)
    return (scales[:, :, None] * levels / 3.0).astype(jnp.bfloat16)

def by_doc(values):
    shaped = values.reshape((RANKS, DOCS, TOK_DEV) + values.shape[1:])
    permuted_axes = (1, 0) + tuple(range(2, shaped.ndim))
    return jnp.transpose(shaped, permuted_axes).reshape((DOCS, DOC_LEN) + values.shape[1:])

def from_doc(values):
    shaped = values.reshape((DOCS, RANKS, TOK_DEV) + values.shape[2:])
    permuted_axes = (1, 0) + tuple(range(2, shaped.ndim))
    return jnp.transpose(shaped, permuted_axes).reshape((TOKENS,) + values.shape[2:])

def head_grads(absorbed_head, rotary_head, upstream_head, latent_doc, keys_doc, place_doc, factor):
    direct = jnp.dot(absorbed_head, latent_doc.T, preferred_element_type=jnp.float32)
    turned = jnp.dot(rotary_head, keys_doc.T, preferred_element_type=jnp.float32)
    visible = place_doc[None, :] <= place_doc[:, None]
    scores = jnp.where(visible, factor * (direct + turned), MASKED)
    maxima = lax.optimization_barrier(jnp.max(scores, axis=1, keepdims=True))
    log_total = maxima + jnp.log(lax.optimization_barrier(jnp.sum(jnp.exp(scores - maxima), axis=1, keepdims=True)))
    softmax = jnp.where(visible, jnp.exp(scores - log_total), 0.0)
    slopes = jnp.dot(upstream_head, latent_doc.T, preferred_element_type=jnp.float32)
    inner_sum = lax.optimization_barrier(jnp.sum(softmax * slopes, axis=1, keepdims=True))
    score_grad = (softmax * (slopes - inner_sum) * factor).astype(jnp.bfloat16)
    softmax_low = softmax.astype(jnp.bfloat16)
    query_part = jnp.dot(score_grad, latent_doc, preferred_element_type=jnp.float32).astype(jnp.bfloat16)
    rotary_part = jnp.dot(score_grad, keys_doc, preferred_element_type=jnp.float32).astype(jnp.bfloat16)
    latent_part = jnp.dot(score_grad.T, absorbed_head, preferred_element_type=jnp.float32)
    latent_part = latent_part + jnp.dot(softmax_low.T, upstream_head, preferred_element_type=jnp.float32)
    keys_part = jnp.dot(score_grad.T, rotary_head, preferred_element_type=jnp.float32)
    return (query_part, rotary_part, latent_part, keys_part)

def reference(query_nope, query_rotary, latent, rotary_keys, output_grad, weight_codes, weight_scale, positions):
    factor = 1.0 / math.sqrt(DN + DR)
    weight = dequant(weight_codes, weight_scale)
    absorbed = jnp.einsum('thn,nhc->thc', query_nope.astype(jnp.float32), weight.astype(jnp.float32)).astype(jnp.bfloat16)
    rotary_query = query_rotary.reshape(TOKENS, HEADS, DR)
    doc_parts = (by_doc(absorbed), by_doc(rotary_query), by_doc(output_grad), by_doc(latent), by_doc(rotary_keys), by_doc(positions))

    def per_document(items):
        absorbed_doc, rotary_doc, upstream_doc, latent_doc, keys_doc, place_doc = items

        def per_head(running, head_items):
            absorbed_head, rotary_head, upstream_head = head_items
            query_part, rotary_part, latent_part, keys_part = head_grads(absorbed_head, rotary_head, upstream_head, latent_doc, keys_doc, place_doc, factor)
            return ((running[0] + latent_part, running[1] + keys_part), (query_part, rotary_part))
        initial = (jnp.zeros((DOC_LEN, DC), jnp.float32), jnp.zeros((DOC_LEN, DR), jnp.float32))
        head_inputs = (jnp.swapaxes(absorbed_doc, 0, 1), jnp.swapaxes(rotary_doc, 0, 1), jnp.swapaxes(upstream_doc, 0, 1))
        summed, stacked = lax.scan(per_head, initial, head_inputs)
        return (summed[0], summed[1], jnp.swapaxes(stacked[0], 0, 1), jnp.swapaxes(stacked[1], 0, 1))
    latent_doc_grad, keys_doc_grad, query_doc_grad, rotary_doc_grad = lax.map(per_document, doc_parts)
    latent_grad = from_doc(latent_doc_grad)
    keys_grad = from_doc(keys_doc_grad)
    dq_latent = from_doc(query_doc_grad)
    rotary_grad = from_doc(rotary_doc_grad).reshape(TOKENS, HEADS * DR)
    query_grad = jnp.einsum('thc,nhc->thn', dq_latent.astype(jnp.float32), weight.astype(jnp.float32)).astype(jnp.bfloat16)
    master_grad = jnp.einsum('thn,thc->nhc', query_nope.astype(jnp.float32), dq_latent.astype(jnp.float32))
    return (query_grad, rotary_grad, latent_grad, keys_grad, master_grad)
```

```python
import math

import jax
import jax.numpy as jnp
from jax import lax
from jax.experimental import pallas as pl
from jax.experimental.pallas import tpu as pltpu
from jax.sharding import Mesh, PartitionSpec as P

RANKS = 8
HEADS = 8
HALF = 64
TOK = 128
DN = 128
DC = 512
DR = 64
WIDE = 640
BLOCK = 256
ROWS = HALF * HEADS
QUARTER = 32
WROWS = 16
FACTOR = 1.0 / math.sqrt(DN + DR)
LOG2E = 1.0 / math.log(2.0)
MASKED = -1e30
VMEM_LIMIT = 56 * 1024 * 1024

bf16 = jnp.bfloat16
f32 = jnp.float32

AXES = ("zl", "x", "c", "zh", "y")
SEQ = ("zl", "x", "c")
HEAD = ("zh", "y")


def nn(a, b):
    return lax.dot_general(a, b, (((1,), (0,)), ((), ())), preferred_element_type=f32)


def nt(a, b):
    return lax.dot_general(a, b, (((1,), (1,)), ((), ())), preferred_element_type=f32)


def tn(a, b):
    return lax.dot_general(a, b, (((0,), (0,)), ((), ())), preferred_element_type=f32)


def iota(shape, axis):
    return lax.broadcasted_iota(jnp.int32, shape, axis)


def chosen(condition):
    return jnp.where(condition, 1.0, 0.0).astype(bf16)


def head_major():
    out, inp = iota((128, 128), 0), iota((128, 128), 1)
    return chosen(inp == (out % 16) * 8 + out // 16)


def token_major():
    out, inp = iota((128, 128), 0), iota((128, 128), 1)
    return chosen(inp == (out % 8) * 16 + out // 8)


def weight_order(row, x, c):
    other, step, rest = row // 64, (row // 16) % 4, row % 16
    return (rest // 2) * 16 + ((x + step) % 4) * 4 + ((c + other) % 2) * 2 + rest % 2


def call(body, outs, ins, scratch=(), flops=0, smem=(), name=None):
    nbytes = sum(math.prod(s.shape) * s.dtype.itemsize for s in list(outs) + list(ins))
    specs = [
        pl.BlockSpec(memory_space=pltpu.SMEM if i in smem else pltpu.VMEM) for i in range(len(ins))
    ]
    return pl.pallas_call(
        body,
        out_shape=outs,
        in_specs=specs,
        out_specs=[pl.BlockSpec(memory_space=pltpu.VMEM) for _ in outs],
        scratch_shapes=list(scratch),
        compiler_params=pltpu.CompilerParams(vmem_limit_bytes=VMEM_LIMIT),
        cost_estimate=pl.CostEstimate(flops=flops, bytes_accessed=nbytes, transcendentals=0),
        name=name,
    )(*ins)


def shape(*dims, dtype=bf16):
    return jax.ShapeDtypeStruct(dims, dtype)


def prepare_kernel(lat_ref, rot_ref, codes_ref, scale_ref, pos_ref, out_ref):
    y = lax.axis_index("y")
    rows = pl.ds(pl.multiple_of(y * QUARTER, QUARTER), QUARTER)
    codes = codes_ref[...]
    levels = codes + (16 * (codes >> 4) + 8) + (64 * (codes >> 6) + 32)
    row = iota((WROWS, DC), 0)
    scale = jnp.zeros((WROWS, DC), f32)
    for i in range(WROWS):
        scale = jnp.where(row == i, scale_ref[i // HEADS, i % HEADS], scale)
    weight = (scale * levels.astype(f32) / 3.0).astype(bf16)
    widen = chosen(iota((DR, 128), 0) == iota((DR, 128), 1))
    lane = iota((QUARTER, 128), 1)
    run = [(pos_ref[half * HALF] >> 6).astype(f32) for half in range(2)]
    rest = nn(rot_ref[rows, :], widen)
    rest = jnp.where(lane == DR, run[0], jnp.where(lane == DR + 1, run[1], rest)).astype(bf16)
    lat = lat_ref[rows, :]
    blank = jnp.zeros((WROWS, 128), bf16)
    for r in range(RANKS):
        out_ref[r, 0:QUARTER, 0:DC] = lat
        out_ref[r, 0:QUARTER, DC:WIDE] = rest
        out_ref[r, QUARTER : QUARTER + WROWS, 0:DC] = weight
        out_ref[r, QUARTER : QUARTER + WROWS, DC:WIDE] = blank


def split_kernel(in_ref, lat_ref, weight_ref):
    for r in range(RANKS):
        lat_ref[r * QUARTER : (r + 1) * QUARTER, :] = in_ref[r, 0:QUARTER, :]
    rows = jnp.concatenate(
        [in_ref[r, QUARTER : QUARTER + WROWS, 0:DC] for r in range(RANKS)], axis=0
    )
    out, inp = iota((128, 128), 0), iota((128, 128), 1)
    head, rank, n = out // 16, (out % 16) // 2, out % 2
    weight_ref[...] = nn(chosen(inp == rank * 16 + n * 8 + head), rows).astype(bf16)


def queries_kernel(nope_ref, rot_ref, up_ref, nope_out, rot_out, up_out):
    x, c = lax.axis_index("x"), lax.axis_index("c")
    by_head = head_major()
    inp, out = iota((DN, DN), 0), iota((DN, DN), 1)
    reorder = chosen(inp == weight_order(out, x, c))
    for g in range(TOK // 16):
        half, start = g // 4, (g % 4) * 16
        rows = slice(g * 128, (g + 1) * 128)
        nope = nn(nn(by_head, nope_ref[rows, :]).astype(bf16), reorder).astype(bf16)
        up = nn(by_head, up_ref[rows, :]).astype(bf16)
        for h in range(HEADS):
            place = (half * HEADS + h) * HALF + start
            nope_out[place : place + 16, :] = nope[h * 16 : (h + 1) * 16, :]
            up_out[place : place + 16, :] = up[h * 16 : (h + 1) * 16, :]
    inp, out = iota((128, 128), 0), iota((128, 128), 1)
    for h in range(HEADS):
        pick = chosen((inp == out + DR * (h % 2)) & (out < DR))
        turned = nn(rot_ref[:, (h // 2) * 128 : (h // 2 + 1) * 128], pick).astype(bf16)
        for half in range(2):
            place = (half * HEADS + h) * HALF
            rot_out[place : place + HALF, :] = turned[half * HALF : (half + 1) * HALF, :]


def attention_kernel(
    runs_ref,
    pos_ref,
    l0,
    l1,
    l2,
    l3,
    w0,
    w1,
    w2,
    w3,
    wo,
    nope_ref,
    rot_ref,
    up_ref,
    k0,
    k1,
    k2,
    k3,
    own_ref,
    other_ref,
    dq_ref,
    weight_ref,
    keys,
    query,
    score,
    slope,
    dkey,
    dquery,
):
    y = lax.axis_index("y")

    def place_of(step, rank):
        quarter = (y + step) % 4
        run = runs_ref[rank * 2 + quarter // 2]
        return pl.ds(pl.multiple_of(run * HALF + (quarter % 2) * QUARTER, QUARTER), QUARTER)

    for step, part in enumerate((l0, l1, l2, l3)):
        for r in range(RANKS):
            keys[place_of(step, r), :] = part[r * QUARTER : (r + 1) * QUARTER, :]
    for h in range(HEADS):
        for step, part in enumerate((w0, w1, w2, w3)):
            weight_ref[h * DN + step * 16 : h * DN + step * 16 + 16, :] = part[
                h * 16 : h * 16 + 16, :
            ]
            at = h * DN + 64 + step * 16
            weight_ref[at : at + 16, :] = wo[step * 128 + h * 16 : step * 128 + h * 16 + 16, :]
    for h in range(HEADS):
        pair = [nope_ref[(half * HEADS + h) * HALF : (half * HEADS + h + 1) * HALF, :] for half in range(2)]
        absorbed = nn(jnp.concatenate(pair, axis=0), weight_ref[h * DN : (h + 1) * DN, :])
        for half in range(2):
            at = (half * HEADS + h) * HALF
            query[at : at + HALF, 0:DC] = absorbed[half * HALF : (half + 1) * HALF, :].astype(bf16)
    query[:, DC:WIDE] = rot_ref[...]
    dkey[...] = jnp.zeros_like(dkey)

    for half in range(2):
        rows = slice(half * ROWS, (half + 1) * ROWS)
        run = pos_ref[half * HALF] >> 6
        place = run * HALF + iota((1, ROWS), 1) % HALF
        count = run // 4 + 1

        def scores(j, top):
            at = pl.ds(pl.multiple_of(j * BLOCK, BLOCK), BLOCK)
            part = keys[at, :]
            s = nt(part, query[rows, :]) * (FACTOR * LOG2E)
            s = jnp.where(j * BLOCK + iota((BLOCK, ROWS), 0) <= place, s, MASKED)
            score[j] = s
            slope[j] = nt(part[:, 0:DC], up_ref[rows, :])
            return jnp.maximum(top, jnp.max(s, axis=0, keepdims=True))

        top = lax.fori_loop(0, count, scores, jnp.full((1, ROWS), MASKED, f32))

        def totals(j, running):
            total, weighted = running
            e = jnp.exp2(score[j] - top)
            score[j] = e
            return (
                total + jnp.sum(e, axis=0, keepdims=True),
                weighted + jnp.sum(e * slope[j], axis=0, keepdims=True),
            )

        zero = jnp.zeros((1, ROWS), f32)
        total, weighted = lax.fori_loop(0, count, totals, (zero, zero))
        inverse = 1.0 / total
        inner = weighted * inverse
        dquery[...] = jnp.zeros_like(dquery)

        def grads(j, carry):
            at = pl.ds(pl.multiple_of(j * BLOCK, BLOCK), BLOCK)
            prob = score[j] * inverse
            grad = (prob * (slope[j] - inner) * FACTOR).astype(bf16)
            dquery[...] += tn(grad, keys[at, :])
            dkey[at, :] += nn(grad, query[rows, :])
            dkey[at, 0:DC] += nn(prob.astype(bf16), up_ref[rows, :])
            return carry

        lax.fori_loop(0, count, grads, 0)
        dq_ref[rows, :] = dquery[...].astype(bf16)

    for step, part in enumerate((k0, k1, k2, k3)):
        for r in range(RANKS):
            part[r * QUARTER : (r + 1) * QUARTER, :] = dkey[place_of(step, r), :].astype(bf16)
    for h in range(HEADS):
        places = [slice((half * HEADS + h) * HALF, (half * HEADS + h + 1) * HALF) for half in range(2)]
        nope = jnp.concatenate([nope_ref[p, :] for p in places], axis=0)
        dq = jnp.concatenate([dq_ref[p, 0:DC] for p in places], axis=0)
        master = tn(nope, dq).astype(bf16)
        for step in range(4):
            at = slice(step * 128 + h * 16, step * 128 + h * 16 + 16)
            own_ref[at, :] = master[step * 16 : step * 16 + 16, :]
            other_ref[at, :] = master[64 + step * 16 : 64 + step * 16 + 16, :]


def query_grads_kernel(dq_ref, weight_ref, nope_out, rot_out, scratch):
    x, c = lax.axis_index("x"), lax.axis_index("c")
    out, inp = iota((DN, DN), 1), iota((DN, DN), 0)
    reorder = chosen(out == weight_order(inp, x, c))
    i, j = iota((128, 128), 0), iota((128, 128), 1)
    left = chosen((i == j) & (j < DR))
    right = chosen((i == j - DR) & (i < DR))
    for h in range(HEADS):
        places = [slice((half * HEADS + h) * HALF, (half * HEADS + h + 1) * HALF) for half in range(2)]
        dq = jnp.concatenate([dq_ref[p, 0:DC] for p in places], axis=0)
        grad = nt(dq, weight_ref[h * DN : (h + 1) * DN, :]).astype(bf16)
        scratch[h * TOK : (h + 1) * TOK, :] = nn(grad, reorder).astype(bf16)
    by_token = token_major()
    for g in range(TOK // 16):
        rows = [scratch[h * TOK + g * 16 : h * TOK + g * 16 + 16, :] for h in range(HEADS)]
        nope_out[g * 128 : (g + 1) * 128, :] = nn(by_token, jnp.concatenate(rows, axis=0)).astype(bf16)
    for p in range(HEADS // 2):
        sides = []
        for h in (2 * p, 2 * p + 1):
            places = [slice((half * HEADS + h) * HALF, (half * HEADS + h + 1) * HALF) for half in range(2)]
            sides.append(jnp.concatenate([dq_ref[q, DC:WIDE] for q in places], axis=0))
        rot_out[:, p * 128 : (p + 1) * 128] = (nn(sides[0], left) + nn(sides[1], right)).astype(bf16)


def core_sum_kernel(own_ref, got_ref, m0, m1, m2, m3):
    for step, part in enumerate((m0, m1, m2, m3)):
        rows = slice(step * 128, (step + 1) * 128)
        part[...] = (own_ref[rows, :].astype(f32) + got_ref[rows, :].astype(f32)).astype(bf16)


def plane_sum_kernel(m0, m1, m2, m3, k0, k1, k2, k3, out_ref):
    master = m0[...].astype(f32) + m1[...].astype(f32) + m2[...].astype(f32) + m3[...].astype(f32)
    out, inp = iota((128, 128), 0), iota((128, 128), 1)
    rank, n, head = out // 16, (out % 16) // 8, out % 8
    master = nn(chosen(inp == head * 16 + rank * 2 + n), master.astype(bf16)).astype(bf16)
    blank = jnp.zeros((WROWS, 128), bf16)
    for r in range(RANKS):
        rows = slice(r * QUARTER, (r + 1) * QUARTER)
        part = k0[rows, :].astype(f32) + k1[rows, :].astype(f32)
        part = part + k2[rows, :].astype(f32) + k3[rows, :].astype(f32)
        out_ref[r, 0:QUARTER, :] = part.astype(bf16)
        out_ref[r, QUARTER : QUARTER + WROWS, 0:DC] = master[r * 16 : r * 16 + 16, :]
        out_ref[r, QUARTER : QUARTER + WROWS, DC:WIDE] = blank


def rank_sum_kernel(in_ref, keys_ref, master_ref):
    keys = in_ref[0, 0:QUARTER, :].astype(f32)
    master = in_ref[0, QUARTER : QUARTER + WROWS, 0:DC].astype(f32)
    for r in range(1, RANKS):
        keys = keys + in_ref[r, 0:QUARTER, :].astype(f32)
        master = master + in_ref[r, QUARTER : QUARTER + WROWS, 0:DC].astype(f32)
    master_ref[...] = master
    keys = keys.astype(bf16)
    for r in range(8):
        keys_ref[r] = keys


def head_sum_kernel(in_ref, latent_ref, rotary_ref):
    for y in range(4):
        rows = slice(y * QUARTER, (y + 1) * QUARTER)
        total = in_ref[y].astype(f32) + in_ref[4 + y].astype(f32)
        latent_ref[rows, :] = total[:, 0:DC]
        rotary_ref[rows, :] = total[:, DC : DC + DR]


def shift(block, axis, step):
    n = lax.axis_size(axis)
    return lax.ppermute(block, axis, [(i, (i + step) % n) for i in range(n)])


def swap(block, axis):
    return lax.ppermute(block, axis, [(0, 1), (1, 0)])


def everyone(blocks, axes):
    return lax.all_to_all(blocks, axes, 0, 0, tiled=True)


def shards(nope, rotary, latent, keys, upstream, codes, scale, positions):
    blocks = (shape(RANKS, QUARTER + WROWS, WIDE),)
    (send,) = call(
        prepare_kernel,
        blocks,
        (latent, keys, codes.reshape(WROWS, DC), scale, positions),
        smem=(3, 4),
        name="prepare",
    )
    got = everyone(send, "zl")
    l0, w0 = call(split_kernel, (shape(256, WIDE), shape(128, DC)), (got,), name="split")
    runs = got[:, 0, DC + DR : DC + DR + 2].astype(jnp.int32).reshape(16)
    w = [w0] + [shift(w0, "x", -step) for step in (1, 3, 2)]
    w = [w[0], w[1], w[3], w[2]]
    lat = [l0] + [shift(l0, "y", -step) for step in (1, 3, 2)]
    lat = [lat[0], lat[1], lat[3], lat[2]]
    wo = swap(jnp.concatenate(w, axis=0), "c")
    nope_rows, rot_rows, up_rows = call(
        queries_kernel,
        (shape(1024, DN), shape(1024, 128), shape(1024, DC)),
        (nope.reshape(1024, DN), rotary, upstream.reshape(1024, DC)),
        flops=2 * 1024 * 128 * 1024,
        name="queries",
    )
    k0, k1, k2, k3, own, other, dq, weight = call(
        attention_kernel,
        (shape(256, WIDE),) * 4 + (shape(512, DC),) * 2 + (shape(1024, WIDE), shape(1024, DC)),
        (runs, positions, *lat, *w, wo, nope_rows, rot_rows, up_rows),
        scratch=(
            pltpu.VMEM((1024, WIDE), bf16),
            pltpu.VMEM((1024, WIDE), bf16),
            pltpu.VMEM((4, BLOCK, ROWS), f32),
            pltpu.VMEM((4, BLOCK, ROWS), f32),
            pltpu.VMEM((1024, WIDE), f32),
            pltpu.VMEM((ROWS, WIDE), f32),
        ),
        smem=(0, 1),
        flops=2 * 512 * 1280 * 2944,
        name="attention",
    )
    got_other = swap(other, "c")
    k = [k0, shift(k1, "y", 1), shift(k3, "y", 3), shift(k2, "y", 2)]
    m0, m1, m2, m3 = call(core_sum_kernel, (shape(128, DC),) * 4, (own, got_other), name="core_sum")
    m = [m0, shift(m1, "x", 1), shift(m3, "x", 3), shift(m2, "x", 2)]
    nope_grad, rot_grad = call(
        query_grads_kernel,
        (shape(1024, DN), shape(TOK, HEADS * DR)),
        (dq, weight),
        scratch=(pltpu.VMEM((1024, DN), bf16),),
        flops=2 * 1024 * 128 * 768,
        name="query_grads",
    )
    (send,) = call(plane_sum_kernel, blocks, (*m, *k), name="plane_sum")
    got = everyone(send, "zl")
    summed, master = call(
        rank_sum_kernel, (shape(8, QUARTER, WIDE), shape(WROWS, DC, dtype=f32)), (got,), name="rank_sum"
    )
    got = everyone(summed, HEAD)
    latent_grad, keys_grad = call(
        head_sum_kernel, (shape(TOK, DC, dtype=f32), shape(TOK, DR, dtype=f32)), (got,), name="head_sum"
    )
    return (
        nope_grad.reshape(TOK, HEADS, DN),
        rot_grad,
        latent_grad,
        keys_grad,
        master.reshape(2, HEADS, DC),
    )


def solution(mesh):
    fine = Mesh(mesh.devices.reshape(8, 4, 2, 2, 4), AXES)
    in_specs = (
        P(SEQ, HEAD, None),
        P(SEQ, HEAD),
        P(SEQ, None),
        P(SEQ, None),
        P(SEQ, HEAD, None),
        P(SEQ, HEAD, None),
        P(SEQ, HEAD),
        P(SEQ),
    )
    out_specs = (
        P(SEQ, HEAD, None),
        P(SEQ, HEAD),
        P(SEQ, None),
        P(SEQ, None),
        P(SEQ, HEAD, None),
    )
    return jax.shard_map(shards, mesh=fine, in_specs=in_specs, out_specs=out_specs, check_vma=False)
```

```python
import math

import jax
import jax.numpy as jnp
from jax import lax
from jax.experimental import pallas as pl
from jax.experimental.pallas import tpu as pltpu
from jax.sharding import Mesh, PartitionSpec as P

RANKS = 8
HEADS = 8
HALF = 64
TOK = 128
DN = 128
DC = 512
DR = 64
WIDE = 640
BLOCK = 256
ROWS = HALF * HEADS
QUARTER = 32
WROWS = 16
FACTOR = 1.0 / math.sqrt(DN + DR)
LOG2E = 1.0 / math.log(2.0)
MASKED = -1e30
MIB = 1024 * 1024

bf16 = jnp.bfloat16
f32 = jnp.float32

AXES = ("zl", "x", "c", "zh", "y")
SEQ = ("zl", "x", "c")
HEAD = ("zh", "y")


def nn(a, b):
    return lax.dot_general(a, b, (((1,), (0,)), ((), ())), preferred_element_type=f32)


def nt(a, b):
    return lax.dot_general(a, b, (((1,), (1,)), ((), ())), preferred_element_type=f32)


def tn(a, b):
    return lax.dot_general(a, b, (((0,), (0,)), ((), ())), preferred_element_type=f32)


def iota(shape, axis):
    return lax.broadcasted_iota(jnp.int32, shape, axis)


def chosen(condition):
    return jnp.where(condition, 1.0, 0.0).astype(bf16)


def head_major():
    out, inp = iota((128, 128), 0), iota((128, 128), 1)
    return chosen(inp == (out % 16) * 8 + out // 16)


def token_major():
    out, inp = iota((128, 128), 0), iota((128, 128), 1)
    return chosen(inp == (out % 8) * 16 + out // 8)


def weight_order(row):
    x, c, rank, n = row // 32, (row // 16) % 2, (row % 16) // 2, row % 2
    return rank * 16 + x * 4 + c * 2 + n


FETCH = (((1, -3), (-1, 3), (2, -2), (4, None)), ((-1, 3), (1, -3), (2, -2), (-4, None)))


FOLD_X = (0, 3, 1, 2)
FOLD = (0, 4, 2, 6, 1, 5, 3, 7)


def call(body, outs, ins, scratch=(), flops=0, smem=(), hbm=(), name=None, vmem=6):
    nbytes = sum(math.prod(s.shape) * s.dtype.itemsize for s in list(outs) + list(ins))
    spaces = [
        pltpu.SMEM if i in smem else pltpu.HBM if i in hbm else pltpu.VMEM for i in range(len(ins))
    ]
    specs = [pl.BlockSpec(memory_space=space) for space in spaces]
    return pl.pallas_call(
        body,
        out_shape=outs,
        in_specs=specs,
        out_specs=[pl.BlockSpec(memory_space=pltpu.VMEM) for _ in outs],
        scratch_shapes=list(scratch),
        compiler_params=pltpu.CompilerParams(vmem_limit_bytes=vmem * MIB),
        cost_estimate=pl.CostEstimate(flops=flops, bytes_accessed=nbytes, transcendentals=0),
        name=name,
    )(*ins)


def shape(*dims, dtype=bf16):
    return jax.ShapeDtypeStruct(dims, dtype)


def prepare_kernel(
    lat_hbm,
    rot_hbm,
    codes_hbm,
    scale_hbm,
    pos_hbm,
    weight_out,
    pack_out,
    rot_ref,
    codes_ref,
    scale_ref,
    pos_ref,
    sems,
):
    pairs = (
        (codes_hbm, codes_ref),
        (scale_hbm, scale_ref),
        (pos_hbm, pos_ref),
        (rot_hbm, rot_ref),
        (lat_hbm, pack_out.at[:, 0:DC]),
    )
    copies = [pltpu.make_async_copy(src, dst, sems.at[i]) for i, (src, dst) in enumerate(pairs)]
    for copy in copies:
        copy.start()
    for copy in copies:
        copy.wait()
    codes = codes_ref[...]
    levels = codes + (16 * (codes >> 4) + 8) + (64 * (codes >> 6) + 32)
    row = iota((WROWS, DC), 0)
    scale = jnp.zeros((WROWS, DC), f32)
    for i in range(WROWS):
        scale = jnp.where(row == i, scale_ref[i // HEADS, i % HEADS], scale)
    weight = (scale * levels.astype(f32) / 3.0).astype(bf16)
    lane = iota((WROWS, 128), 1)
    run = [(pos_ref[half * HALF] >> 6).astype(f32) for half in range(2)]
    rest = jnp.where(lane == 0, run[0], jnp.where(lane == 1, run[1], 0.0)).astype(bf16)
    for r in range(RANKS):
        weight_out[r, :, 0:DC] = weight
        weight_out[r, :, DC:WIDE] = rest
    widen = chosen(iota((DR, 128), 0) == iota((DR, 128), 1))
    pack_out[:, DC:WIDE] = tn(rot_ref[...], widen).astype(bf16)


def spread_weight_kernel(in_ref, out_ref):
    out, inp = iota((128, 128), 0), iota((128, 128), 1)
    head, rank, n = out // 16, (out % 16) // 2, out % 2
    weight = nn(chosen(inp == rank * 16 + n * 8 + head), in_ref[:, 0:DC]).astype(bf16)
    for i in range(8):
        out_ref[i] = weight


def join_kernel(first, second, out_ref):
    out_ref[0:TOK, :] = first[...]
    out_ref[TOK : 2 * TOK, :] = second[...]


def order_queries(nope_ref, rot_ref, up_ref, nope_out, query, up_out):
    by_head = head_major()
    inp, out = iota((DN, DN), 0), iota((DN, DN), 1)
    reorder = chosen(inp == weight_order(out))
    for g in range(TOK // 16):
        half, start = g // 4, (g % 4) * 16
        rows = slice(g * 128, (g + 1) * 128)
        nope = nn(nn(by_head, nope_ref[rows, :]).astype(bf16), reorder).astype(bf16)
        up = nn(by_head, up_ref[rows, :]).astype(bf16)
        for h in range(HEADS):
            place = (half * HEADS + h) * HALF + start
            nope_out[place : place + 16, :] = nope[h * 16 : (h + 1) * 16, :]
            up_out[place : place + 16, :] = up[h * 16 : (h + 1) * 16, :]
    for h in range(HEADS):
        pick = chosen((inp == out + DR * (h % 2)) & (out < DR))
        turned = nn(rot_ref[:, (h // 2) * 128 : (h // 2 + 1) * 128], pick).astype(bf16)
        for half in range(2):
            place = (half * HEADS + h) * HALF
            query[place : place + HALF, DC:WIDE] = turned[half * HALF : (half + 1) * HALF, :]


def attention_kernel(
    runs_ref,
    pos_ref,
    pack_ref,
    l0,
    l1,
    l2,
    l3,
    w_ref,
    nope_in,
    rot_in,
    up_in,
    k0,
    k1,
    k2,
    k3,
    own_out,
    other_out,
    dq_ref,
    weight_ref,
    keys,
    query,
    score,
    slope,
    dkey,
    dquery,
    nope_ref,
    up_ref,
    staged,
):
    order_queries(nope_in, rot_in, up_in, nope_ref, query, up_ref)
    zl, c, y = lax.axis_index("zl"), lax.axis_index("c"), lax.axis_index("y")
    x = lax.axis_index("x")

    def place_of(run, start, size):
        return pl.ds(pl.multiple_of(run * HALF + start, size), size)

    for half in range(2):
        run = pos_ref[half * HALF] >> 6
        keys[place_of(run, 0, HALF), :] = pack_ref[half * HALF : (half + 1) * HALF, :]
    for step, part in enumerate((l0, l1, l2, l3)):
        source = (y + step) % 4
        for slot in range(2):
            away = jnp.int32(0)
            for core in range(2):
                for owner in range(4):
                    here = (c == core) & (source == owner)
                    away = jnp.where(here, FETCH[core][owner][slot] or 0, away)

            @pl.when(away != 0)
            def _():
                rank = (zl + RANKS + away) % RANKS
                for half in range(2):
                    run = runs_ref[rank * 2 + half]
                    start = slot * TOK + half * HALF
                    keys[place_of(run, 0, HALF), :] = part[start : start + HALF, :]

    for h in range(HEADS):
        for i in range(8):
            weight_ref[h * DN + i * 16 : h * DN + i * 16 + 16, :] = w_ref[i, h * 16 : h * 16 + 16, :]
    for h in range(HEADS):
        pair = [nope_ref[(half * HEADS + h) * HALF : (half * HEADS + h + 1) * HALF, :] for half in range(2)]
        absorbed = nn(jnp.concatenate(pair, axis=0), weight_ref[h * DN : (h + 1) * DN, :])
        for half in range(2):
            at = (half * HEADS + h) * HALF
            query[at : at + HALF, 0:DC] = absorbed[half * HALF : (half + 1) * HALF, :].astype(bf16)
    dkey[...] = jnp.zeros_like(dkey)

    for half in range(2):
        rows = slice(half * ROWS, (half + 1) * ROWS)
        run = pos_ref[half * HALF] >> 6
        place = run * HALF + iota((1, ROWS), 1) % HALF
        count = run // 4 + 1

        def scores(j, top):
            at = pl.ds(pl.multiple_of(j * BLOCK, BLOCK), BLOCK)
            part = keys[at, :]
            s = nt(part, query[rows, :]) * (FACTOR * LOG2E)
            s = jnp.where(j * BLOCK + iota((BLOCK, ROWS), 0) <= place, s, MASKED)
            score[j] = s
            slope[j] = nt(part[:, 0:DC], up_ref[rows, :])
            return jnp.maximum(top, jnp.max(s, axis=0, keepdims=True))

        top = lax.fori_loop(0, count, scores, jnp.full((1, ROWS), MASKED, f32))

        def totals(j, running):
            total, weighted = running
            e = jnp.exp2(score[j] - top)
            score[j] = e
            return (
                total + jnp.sum(e, axis=0, keepdims=True),
                weighted + jnp.sum(e * slope[j], axis=0, keepdims=True),
            )

        zero = jnp.zeros((1, ROWS), f32)
        total, weighted = lax.fori_loop(0, count, totals, (zero, zero))
        inverse = 1.0 / total
        inner = weighted * inverse
        dquery[...] = jnp.zeros_like(dquery)

        def grads(j, carry):
            at = pl.ds(pl.multiple_of(j * BLOCK, BLOCK), BLOCK)
            prob = score[j] * inverse
            grad = (prob * (slope[j] - inner) * FACTOR).astype(bf16)
            dquery[...] += tn(grad, keys[at, :])
            dkey[at, :] += nn(grad, query[rows, :])
            dkey[at, 0:DC] += nn(prob.astype(bf16), up_ref[rows, :])
            return carry

        lax.fori_loop(0, count, grads, 0)
        dq_ref[rows, :] = dquery[...].astype(bf16)

    for step, part in enumerate((k0, k1, k2, k3)):
        quarter = (y + step) % 4
        for k in range(RANKS):
            run = runs_ref[(zl ^ FOLD[k]) * 2 + quarter // 2]
            at = place_of(run, (quarter % 2) * QUARTER, QUARTER)
            part[k * QUARTER : (k + 1) * QUARTER, :] = dkey[at, :].astype(bf16)
    for h in range(HEADS):
        places = [slice((half * HEADS + h) * HALF, (half * HEADS + h + 1) * HALF) for half in range(2)]
        nope = jnp.concatenate([nope_ref[p, :] for p in places], axis=0)
        dq = jnp.concatenate([dq_ref[p, 0:DC] for p in places], axis=0)
        master = tn(nope, dq).astype(bf16)
        staged[...] = master
        for core, part in enumerate((own_out, other_out)):
            for k, away in enumerate(FOLD_X):
                at = pl.ds(pl.multiple_of(((x ^ away) * 2 + (c + core) % 2) * 16, 16), 16)
                part[k * 128 + h * 16 : k * 128 + h * 16 + 16, :] = staged[at, :]


def query_grads_kernel(dq_ref, weight_ref, nope_out, rot_out, scratch):
    out, inp = iota((DN, DN), 1), iota((DN, DN), 0)
    reorder = chosen(out == weight_order(inp))
    i, j = iota((128, 128), 0), iota((128, 128), 1)
    left = chosen((i == j) & (j < DR))
    right = chosen((i == j - DR) & (i < DR))
    for h in range(HEADS):
        places = [slice((half * HEADS + h) * HALF, (half * HEADS + h + 1) * HALF) for half in range(2)]
        dq = jnp.concatenate([dq_ref[p, 0:DC] for p in places], axis=0)
        grad = nt(dq, weight_ref[h * DN : (h + 1) * DN, :]).astype(bf16)
        scratch[h * TOK : (h + 1) * TOK, :] = nn(grad, reorder).astype(bf16)
    by_token = token_major()
    for g in range(TOK // 16):
        rows = [scratch[h * TOK + g * 16 : h * TOK + g * 16 + 16, :] for h in range(HEADS)]
        nope_out[g * 128 : (g + 1) * 128, :] = nn(by_token, jnp.concatenate(rows, axis=0)).astype(bf16)
    for p in range(HEADS // 2):
        sides = []
        for h in (2 * p, 2 * p + 1):
            places = [slice((half * HEADS + h) * HALF, (half * HEADS + h + 1) * HALF) for half in range(2)]
            sides.append(jnp.concatenate([dq_ref[q, DC:WIDE] for q in places], axis=0))
        rot_out[:, p * 128 : (p + 1) * 128] = (nn(sides[0], left) + nn(sides[1], right)).astype(bf16)


def total_of(parts):
    total = parts[0].astype(f32)
    for part in parts[1:]:
        total = total + part.astype(f32)
    return total


def keys_plane_kernel(k0, k1, k2, k3, keep_ref, send_ref):
    total = total_of([k[...] for k in (k0, k1, k2, k3)])
    keep_ref[...] = total[0:128, :]
    send_ref[...] = total[128:256, :].astype(bf16)


def keys_pair_kernel(keep_ref, got_ref, both_out):
    both_out[...] = (keep_ref[...] + got_ref[...].astype(f32)).astype(bf16)


def keys_cross_kernel(both_ref, got_ref, keep_out, send_out):
    low, high = slice(0, QUARTER), slice(QUARTER, 2 * QUARTER)
    keep_out[...] = total_of([both_ref[low, :], got_ref[high, :]]).astype(bf16)
    send_out[...] = total_of([both_ref[high, :], got_ref[low, :]]).astype(bf16)


def keys_sum_kernel(keep_ref, got_ref, out_ref):
    keys = total_of([keep_ref[...], got_ref[...]]).astype(bf16)
    for y in range(4):
        out_ref[y] = keys


def keys_last_kernel(in_ref, latent_ref, rotary_ref):
    rest = []
    for y in range(4):
        part = in_ref[y].astype(f32)
        latent_ref[y * QUARTER : (y + 1) * QUARTER, :] = part[:, 0:DC]
        rest.append(part[:, DC:WIDE])
    rotary_ref[...] = jnp.concatenate(rest, axis=0).T[0:DR, :]


def master_plane_kernel(own_ref, got_ref, keep_ref, send_ref):
    total = own_ref[...].astype(f32) + got_ref[...].astype(f32)
    keep_ref[...] = total[0:256, :]
    send_ref[...] = total[256:512, :].astype(bf16)


def master_order_kernel(keep_ref, got_ref, keep_out, send_out):
    master = (keep_ref[...] + got_ref[...].astype(f32)).astype(bf16)
    zl = lax.axis_index("zl")
    out, inp = iota((128, 128), 0), iota((128, 128), 1)
    k, n, head = out // 16, (out % 16) // 8, out % 8
    rank = zl ^ ((k % 2) * 4 + ((k // 2) % 2) * 2 + k // 4)
    master = nn(chosen(inp == head * 16 + rank * 2 + n), master)
    keep_out[...] = master[0:64, :]
    send_out[...] = master[64:128, :].astype(bf16)


def fold_kernel(keep_ref, got_ref, keep_out, send_out):
    size = keep_out.shape[0]
    keep_out[...] = keep_ref[0:size, :] + got_ref[0:size, :].astype(f32)
    send_out[...] = (keep_ref[size:, :] + got_ref[size:, :].astype(f32)).astype(bf16)


def master_last_kernel(keep_ref, got_ref, out_ref):
    out_ref[...] = keep_ref[...] + got_ref[...].astype(f32)


def fetch(block, slot):
    axes, sizes = ("zl", "c", "zh", "y"), (8, 2, 2, 4)
    pairs = []
    for place in range(16):
        for c in range(2):
            for y in range(4):
                step = FETCH[c][y][slot]
                if step is not None:
                    ends = []
                    for z in ((place + step) % 16, place):
                        ends.append((((z % 8) * 2 + c) * 2 + z // 8) * 4 + y)
                    pairs.append(tuple(ends))
    return lax.ppermute(block, axes, pairs)


def shift(block, axis, step):
    n = lax.axis_size(axis)
    return lax.ppermute(block, axis, [(i, (i + step) % n) for i in range(n)])


def across(block, axis, step):
    n = lax.axis_size(axis)
    return lax.ppermute(block, axis, [(i, i ^ step) for i in range(n)])


def over_edge(block):
    def partner(place):
        return (place + (4 if place % 8 >= 4 else -4)) % 16

    def index(place):
        return place % 8 * 2 + place // 8

    return lax.ppermute(block, ("zl", "zh"), [(index(p), index(partner(p))) for p in range(16)])


def everyone(blocks, axes):
    return lax.all_to_all(blocks, axes, 0, 0, tiled=True)


def shards(nope, rotary, latent, keys, upstream, codes, scale, positions):
    weight_send, pack = call(
        prepare_kernel,
        (shape(RANKS, WROWS, WIDE), shape(TOK, WIDE)),
        (latent, keys.T, codes.reshape(WROWS, DC), scale, positions),
        scratch=(
            pltpu.VMEM((DR, TOK), bf16),
            pltpu.VMEM((WROWS, DC), jnp.int32),
            pltpu.SMEM((2, HEADS), f32),
            pltpu.SMEM((TOK,), jnp.int32),
            pltpu.SemaphoreType.DMA((5,)),
        ),
        hbm=(0, 1, 2, 3, 4),
        name="prepare",
        vmem=56,
    )
    weight_ranks = everyone(weight_send, "zl")
    first, second = fetch(pack, 0), fetch(pack, 1)
    weight_ranks, first, second = lax.optimization_barrier((weight_ranks, first, second))
    (weight_spread,) = call(
        spread_weight_kernel,
        (shape(8, 128, DC),),
        (weight_ranks.reshape(128, WIDE),),
        name="spread_weight",
    )
    weight_all = everyone(weight_spread, ("x", "c"))
    (joined,) = call(join_kernel, (shape(2 * TOK, WIDE),), (first, second), name="join")
    lat = [joined] + [shift(joined, "y", -step) for step in (1, 2, 3)]
    runs = weight_ranks[:, 0, DC : DC + 2].astype(jnp.int32).reshape(16)
    k0, k1, k2, k3, own, other, dq, weight = call(
        attention_kernel,
        (shape(256, WIDE),) * 4 + (shape(512, DC),) * 2 + (shape(1024, WIDE), shape(1024, DC)),
        (
            runs,
            positions,
            pack,
            *lat,
            weight_all,
            nope.reshape(1024, DN),
            rotary,
            upstream.reshape(1024, DC),
        ),
        scratch=(
            pltpu.VMEM((1024, WIDE), bf16),
            pltpu.VMEM((1024, WIDE), bf16),
            pltpu.VMEM((4, BLOCK, ROWS), f32),
            pltpu.VMEM((4, BLOCK, ROWS), f32),
            pltpu.VMEM((1024, WIDE), f32),
            pltpu.VMEM((ROWS, WIDE), f32),
            pltpu.VMEM((1024, DN), bf16),
            pltpu.VMEM((1024, DC), bf16),
            pltpu.VMEM((DN, DC), bf16),
        ),
        smem=(0, 1),
        flops=2 * 512 * 1280 * 2944,
        name="attention",
        vmem=56,
    )
    k = [k0] + [shift(part, "y", step) for step, part in ((1, k1), (2, k2), (3, k3))]
    other = across(other, "c", 1)
    nope_grad, rot_grad = call(
        query_grads_kernel,
        (shape(1024, DN), shape(TOK, HEADS * DR)),
        (dq, weight),
        scratch=(pltpu.VMEM((1024, DN), bf16),),
        flops=2 * 1024 * 128 * 768,
        name="query_grads",
    )
    def folded(body, size, width, ins, dtype=f32, name="fold"):
        return call(body, (shape(size, width, dtype=dtype), shape(size, width)), ins, name=name)

    together = lax.optimization_barrier
    mkeep, send = folded(master_plane_kernel, 256, DC, (own, other), name="master_plane")
    got = across(send, "x", 1)
    keep, send = folded(keys_plane_kernel, 128, WIDE, k, name="keys_plane")
    got, mgot = together((across(send, "zl", 1), got))
    mkeep, msend = folded(fold_kernel, 128, DC, (mkeep, mgot))
    keep, send = folded(fold_kernel, 64, WIDE, (keep, got))
    got, mgot = together((across(send, "zl", 2), across(msend, "x", 3)))
    mkeep, msend = folded(master_order_kernel, 64, DC, (mkeep, mgot), name="master_order")
    (both,) = call(keys_pair_kernel, (shape(64, WIDE),), (keep, got), name="keys_pair")
    got, mgot = together((across(both, "zl", 4), across(msend, "zl", 1)))
    mkeep, msend = folded(fold_kernel, 32, DC, (mkeep, mgot))
    keep, send = folded(keys_cross_kernel, QUARTER, WIDE, (both, got), dtype=bf16, name="keys_cross")
    got, mgot = together((over_edge(send), across(msend, "zl", 2)))
    mkeep, msend = folded(fold_kernel, 16, DC, (mkeep, mgot))
    (dkey_sum,) = call(keys_sum_kernel, (shape(4, QUARTER, WIDE),), (keep, got), name="keys_sum")
    dkey_all, mgot = together((everyone(dkey_sum, "y"), across(msend, "zl", 4)))
    (master_grad,) = call(
        master_last_kernel, (shape(WROWS, DC, dtype=f32),), (mkeep, mgot), name="master_last"
    )
    latent_grad, keys_grad = call(
        keys_last_kernel,
        (shape(TOK, DC, dtype=f32), shape(DR, TOK, dtype=f32)),
        (dkey_all,),
        name="keys_last",
    )
    return (
        nope_grad.reshape(TOK, HEADS, DN),
        rot_grad,
        latent_grad,
        keys_grad.T,
        master_grad.reshape(2, HEADS, DC),
    )


def solution(mesh):
    fine = Mesh(mesh.devices.reshape(8, 4, 2, 2, 4), AXES)
    in_specs = (
        P(SEQ, HEAD, None),
        P(SEQ, HEAD),
        P(SEQ, None),
        P(SEQ, None),
        P(SEQ, HEAD, None),
        P(SEQ, HEAD, None),
        P(SEQ, HEAD),
        P(SEQ),
    )
    out_specs = (
        P(SEQ, HEAD, None),
        P(SEQ, HEAD),
        P(SEQ, None),
        P(SEQ, None),
        P(SEQ, HEAD, None),
    )
    return jax.shard_map(shards, mesh=fine, in_specs=in_specs, out_specs=out_specs, check_vma=False)
```

```python
import math

import jax
import jax.numpy as jnp
from jax import lax
from jax.experimental import pallas as pl
from jax.experimental.pallas import tpu as pltpu
from jax.sharding import Mesh, PartitionSpec as P

RANKS = 8
HEADS = 8
HALF = 64
TOK = 128
DN = 128
DC = 512
DR = 64
WIDE = 640
BLOCK = 256
ROWS = HALF * HEADS
QUARTER = 32
WROWS = 16
FACTOR = 1.0 / math.sqrt(DN + DR)
LOG2E = 1.0 / math.log(2.0)
MASKED = -1e30
MIB = 1024 * 1024

bf16 = jnp.bfloat16
f32 = jnp.float32

AXES = ("zl", "x", "c", "zh", "y")
SEQ = ("zl", "x", "c")
HEAD = ("zh", "y")


def nn(a, b):
    return lax.dot_general(a, b, (((1,), (0,)), ((), ())), preferred_element_type=f32)


def nt(a, b):
    return lax.dot_general(a, b, (((1,), (1,)), ((), ())), preferred_element_type=f32)


def tn(a, b):
    return lax.dot_general(a, b, (((0,), (0,)), ((), ())), preferred_element_type=f32)


def iota(shape, axis):
    return lax.broadcasted_iota(jnp.int32, shape, axis)


def chosen(condition):
    return jnp.where(condition, 1.0, 0.0).astype(bf16)


def head_major():
    out, inp = iota((128, 128), 0), iota((128, 128), 1)
    return chosen(inp == (out % 16) * 8 + out // 16)


def token_major():
    out, inp = iota((128, 128), 0), iota((128, 128), 1)
    return chosen(inp == (out % 8) * 16 + out // 8)


def weight_order(row):
    x, c = lax.axis_index("x"), lax.axis_index("c")
    core, step, rank, n = c ^ (row // 64), (row // 16) % 4, (row % 16) // 2, row % 2
    return rank * 16 + (x ^ step ^ (step // 2)) * 4 + core * 2 + n


FETCH = (((1, -3), (-1, 3), (2, -2), (4, None)), ((-1, 3), (1, -3), (2, -2), (-4, None)))


FOLD_X = (0, 2, 1, 3)


def call(body, outs, ins, scratch=(), flops=0, smem=(), hbm=(), name=None, vmem=6):
    nbytes = sum(math.prod(s.shape) * s.dtype.itemsize for s in list(outs) + list(ins))
    spaces = [
        pltpu.SMEM if i in smem else pltpu.HBM if i in hbm else pltpu.VMEM for i in range(len(ins))
    ]
    specs = [pl.BlockSpec(memory_space=space) for space in spaces]
    return pl.pallas_call(
        body,
        out_shape=outs,
        in_specs=specs,
        out_specs=[pl.BlockSpec(memory_space=pltpu.VMEM) for _ in outs],
        scratch_shapes=list(scratch),
        compiler_params=pltpu.CompilerParams(vmem_limit_bytes=vmem * MIB),
        cost_estimate=pl.CostEstimate(flops=flops, bytes_accessed=nbytes, transcendentals=0),
        name=name,
    )(*ins)


def shape(*dims, dtype=bf16):
    return jax.ShapeDtypeStruct(dims, dtype)


def prepare_kernel(
    lat_hbm,
    rot_hbm,
    codes_hbm,
    scale_hbm,
    pos_hbm,
    weight_out,
    pack_out,
    rot_ref,
    codes_ref,
    scale_ref,
    pos_ref,
    sems,
):
    pairs = (
        (codes_hbm, codes_ref),
        (scale_hbm, scale_ref),
        (pos_hbm, pos_ref),
        (rot_hbm, rot_ref),
        (lat_hbm, pack_out.at[:, 0:DC]),
    )
    copies = [pltpu.make_async_copy(src, dst, sems.at[i]) for i, (src, dst) in enumerate(pairs)]
    for copy in copies:
        copy.start()
    for copy in copies:
        copy.wait()
    codes = codes_ref[...]
    levels = codes + (16 * (codes >> 4) + 8) + (64 * (codes >> 6) + 32)
    row = iota((WROWS, DC), 0)
    scale = jnp.zeros((WROWS, DC), f32)
    for i in range(WROWS):
        scale = jnp.where(row == i, scale_ref[i // HEADS, i % HEADS], scale)
    weight = (scale * levels.astype(f32) / 3.0).astype(bf16)
    lane = iota((WROWS, 128), 1)
    run = [(pos_ref[half * HALF] >> 6).astype(f32) for half in range(2)]
    rest = jnp.where(lane == 0, run[0], jnp.where(lane == 1, run[1], 0.0)).astype(bf16)
    for r in range(RANKS):
        weight_out[r, :, 0:DC] = weight
        weight_out[r, :, DC:WIDE] = rest
    widen = chosen(iota((DR, 128), 0) == iota((DR, 128), 1))
    pack_out[:, DC:WIDE] = tn(rot_ref[...], widen).astype(bf16)


def order_weight_kernel(in_ref, out_ref):
    out, inp = iota((128, 128), 0), iota((128, 128), 1)
    head, rank, n = out // 16, (out % 16) // 2, out % 2
    out_ref[...] = nn(chosen(inp == rank * 16 + n * 8 + head), in_ref[:, 0:DC]).astype(bf16)


def join_kernel(first, second, out_ref):
    size = first.shape[0]
    out_ref[0:size, :] = first[...]
    out_ref[size : 2 * size, :] = second[...]


def spread_latent_kernel(first, second, out_ref):
    for y in range(4):
        out_ref[y, 0:TOK, :] = first[...]
        out_ref[y, TOK : 2 * TOK, :] = second[...]


def order_queries(nope_ref, rot_ref, up_ref, nope_out, query, up_out):
    by_head = head_major()
    inp, out = iota((DN, DN), 0), iota((DN, DN), 1)
    reorder = chosen(inp == weight_order(out))
    for g in range(TOK // 16):
        half, start = g // 4, (g % 4) * 16
        rows = slice(g * 128, (g + 1) * 128)
        nope = nn(nn(by_head, nope_ref[rows, :]).astype(bf16), reorder).astype(bf16)
        up = nn(by_head, up_ref[rows, :]).astype(bf16)
        for h in range(HEADS):
            place = (half * HEADS + h) * HALF + start
            nope_out[place : place + 16, :] = nope[h * 16 : (h + 1) * 16, :]
            up_out[place : place + 16, :] = up[h * 16 : (h + 1) * 16, :]
    for h in range(HEADS):
        pick = chosen((inp == out + DR * (h % 2)) & (out < DR))
        turned = nn(rot_ref[:, (h // 2) * 128 : (h // 2 + 1) * 128], pick).astype(bf16)
        for half in range(2):
            place = (half * HEADS + h) * HALF
            query[place : place + HALF, DC:WIDE] = turned[half * HALF : (half + 1) * HALF, :]


def attention_kernel(
    runs_ref,
    pos_ref,
    pack_ref,
    lat_ref,
    w_own,
    w_other,
    nope_in,
    rot_in,
    up_in,
    dkey_out,
    own_out,
    other_out,
    dq_ref,
    weight_ref,
    keys,
    query,
    score,
    slope,
    dkey,
    dquery,
    nope_ref,
    up_ref,
):
    order_queries(nope_in, rot_in, up_in, nope_ref, query, up_ref)
    zl, c = lax.axis_index("zl"), lax.axis_index("c")

    def place_of(run, start, size):
        return pl.ds(pl.multiple_of(run * HALF + start, size), size)

    for half in range(2):
        run = pos_ref[half * HALF] >> 6
        keys[place_of(run, 0, HALF), :] = pack_ref[half * HALF : (half + 1) * HALF, :]
    for y in range(4):
        for slot in range(2):
            steps = [FETCH[core][y][slot] for core in range(2)]
            if steps[0] is None:
                continue
            rank = (zl + RANKS + jnp.where(c == 0, steps[0], steps[1])) % RANKS
            for half in range(2):
                start = slot * TOK + half * HALF
                at = place_of(runs_ref[rank * 2 + half], 0, HALF)
                keys[at, :] = lat_ref[y, start : start + HALF, :]
    for h in range(HEADS):
        for core, part in enumerate((w_own, w_other)):
            for step in range(4):
                at = h * DN + core * 64 + step * 16
                place = step * 128 + h * 16
                weight_ref[at : at + 16, :] = part[place : place + 16, :]
    for h in range(HEADS):
        pair = [nope_ref[(half * HEADS + h) * HALF : (half * HEADS + h + 1) * HALF, :] for half in range(2)]
        absorbed = nn(jnp.concatenate(pair, axis=0), weight_ref[h * DN : (h + 1) * DN, :])
        for half in range(2):
            at = (half * HEADS + h) * HALF
            query[at : at + HALF, 0:DC] = absorbed[half * HALF : (half + 1) * HALF, :].astype(bf16)
    dkey[...] = jnp.zeros_like(dkey)

    for half in range(2):
        rows = slice(half * ROWS, (half + 1) * ROWS)
        run = pos_ref[half * HALF] >> 6
        place = run * HALF + iota((1, ROWS), 1) % HALF
        count = run // 4 + 1

        def scores(j, top):
            at = pl.ds(pl.multiple_of(j * BLOCK, BLOCK), BLOCK)
            part = keys[at, :]
            s = nt(part, query[rows, :]) * (FACTOR * LOG2E)
            s = jnp.where(j * BLOCK + iota((BLOCK, ROWS), 0) <= place, s, MASKED)
            score[j] = s
            slope[j] = nt(part[:, 0:DC], up_ref[rows, :])
            return jnp.maximum(top, jnp.max(s, axis=0, keepdims=True))

        top = lax.fori_loop(0, count, scores, jnp.full((1, ROWS), MASKED, f32))

        def totals(j, running):
            total, weighted = running
            e = jnp.exp2(score[j] - top)
            score[j] = e
            return (
                total + jnp.sum(e, axis=0, keepdims=True),
                weighted + jnp.sum(e * slope[j], axis=0, keepdims=True),
            )

        zero = jnp.zeros((1, ROWS), f32)
        total, weighted = lax.fori_loop(0, count, totals, (zero, zero))
        inverse = 1.0 / total
        inner = weighted * inverse
        dquery[...] = jnp.zeros_like(dquery)

        def grads(j, carry):
            at = pl.ds(pl.multiple_of(j * BLOCK, BLOCK), BLOCK)
            prob = score[j] * inverse
            grad = (prob * (slope[j] - inner) * FACTOR).astype(bf16)
            dquery[...] += tn(grad, keys[at, :])
            dkey[at, :] += nn(grad, query[rows, :])
            dkey[at, 0:DC] += nn(prob.astype(bf16), up_ref[rows, :])
            return carry

        lax.fori_loop(0, count, grads, 0)
        dq_ref[rows, :] = dquery[...].astype(bf16)

    for quarter in range(4):
        for k in range(RANKS):
            run = runs_ref[((zl & 4) ^ k) * 2 + quarter // 2]
            at = place_of(run, (quarter % 2) * QUARTER, QUARTER)
            dkey_out[quarter, k * QUARTER : (k + 1) * QUARTER, :] = dkey[at, :].astype(bf16)
    for h in range(HEADS):
        places = [slice((half * HEADS + h) * HALF, (half * HEADS + h + 1) * HALF) for half in range(2)]
        nope = jnp.concatenate([nope_ref[p, :] for p in places], axis=0)
        dq = jnp.concatenate([dq_ref[p, 0:DC] for p in places], axis=0)
        master = tn(nope, dq).astype(bf16)
        for core, part in enumerate((own_out, other_out)):
            for k, step in enumerate(FOLD_X):
                at = core * 64 + step * 16
                part[k * 128 + h * 16 : k * 128 + h * 16 + 16, :] = master[at : at + 16, :]


def query_grads_kernel(dq_ref, weight_ref, nope_out, rot_out, scratch):
    out, inp = iota((DN, DN), 1), iota((DN, DN), 0)
    reorder = chosen(out == weight_order(inp))
    i, j = iota((128, 128), 0), iota((128, 128), 1)
    left = chosen((i == j) & (j < DR))
    right = chosen((i == j - DR) & (i < DR))
    for h in range(HEADS):
        places = [slice((half * HEADS + h) * HALF, (half * HEADS + h + 1) * HALF) for half in range(2)]
        dq = jnp.concatenate([dq_ref[p, 0:DC] for p in places], axis=0)
        grad = nt(dq, weight_ref[h * DN : (h + 1) * DN, :]).astype(bf16)
        scratch[h * TOK : (h + 1) * TOK, :] = nn(grad, reorder).astype(bf16)
    by_token = token_major()
    for g in range(TOK // 16):
        rows = [scratch[h * TOK + g * 16 : h * TOK + g * 16 + 16, :] for h in range(HEADS)]
        nope_out[g * 128 : (g + 1) * 128, :] = nn(by_token, jnp.concatenate(rows, axis=0)).astype(bf16)
    for p in range(HEADS // 2):
        sides = []
        for h in (2 * p, 2 * p + 1):
            places = [slice((half * HEADS + h) * HALF, (half * HEADS + h + 1) * HALF) for half in range(2)]
            sides.append(jnp.concatenate([dq_ref[q, DC:WIDE] for q in places], axis=0))
        rot_out[:, p * 128 : (p + 1) * 128] = (nn(sides[0], left) + nn(sides[1], right)).astype(bf16)


def total_of(parts):
    total = parts[0].astype(f32)
    for part in parts[1:]:
        total = total + part.astype(f32)
    return total


def master_plane_kernel(own_ref, got_ref, keep_ref, send_ref):
    total = own_ref[...].astype(f32) + got_ref[...].astype(f32)
    keep_ref[...] = total[0:256, :]
    send_ref[...] = total[256:512, :].astype(bf16)


def fold_kernel(keep_ref, got_ref, keep_out, send_out):
    size = keep_out.shape[0]
    keep_out[...] = keep_ref[0:size, :] + got_ref[0:size, :].astype(f32)
    send_out[...] = (keep_ref[size:, :] + got_ref[size:, :].astype(f32)).astype(bf16)


def plane_kernel(dkey_ref, keep_ref, got_ref, out_ref):
    keys = total_of([dkey_ref[y] for y in range(4)]).astype(bf16)
    master = (keep_ref[...] + got_ref[...].astype(f32)).astype(bf16)
    zl = lax.axis_index("zl")
    out, inp = iota((128, 128), 0), iota((128, 128), 1)
    rank, n, head = (out // 16) ^ (zl & 4), (out % 16) // 8, out % 8
    master = nn(chosen(inp == head * 16 + rank * 2 + n), master).astype(bf16)
    blank = jnp.zeros((2 * WROWS, 128), bf16)
    for j in range(4):
        for pair in range(2):
            k = pair * 4 + j
            out_ref[j, pair * QUARTER : (pair + 1) * QUARTER, :] = keys[k * QUARTER : (k + 1) * QUARTER, :]
            at = 2 * QUARTER + pair * WROWS
            out_ref[j, at : at + WROWS, 0:DC] = master[k * WROWS : (k + 1) * WROWS, :]
        out_ref[j, 2 * QUARTER :, DC:WIDE] = blank


def quad_sum_kernel(in_ref, both_out, keep_out):
    total = total_of([in_ref[j] for j in range(4)])
    both_out[0 : 2 * QUARTER, :] = total[0 : 2 * QUARTER, :].astype(bf16)
    both_out[2 * QUARTER :, :] = total[2 * QUARTER + WROWS :, :].astype(bf16)
    keep_out[...] = total[2 * QUARTER : 2 * QUARTER + WROWS, 0:DC]


def cross_kernel(both_ref, got_ref, master_ref, keep_out, send_out, master_out):
    low, high = slice(0, QUARTER), slice(QUARTER, 2 * QUARTER)
    keep_out[...] = total_of([both_ref[low, :], got_ref[high, :]]).astype(bf16)
    send_out[...] = total_of([both_ref[high, :], got_ref[low, :]]).astype(bf16)
    master_out[...] = master_ref[...] + got_ref[2 * QUARTER :, 0:DC].astype(f32)


def keys_sum_kernel(keep_ref, got_ref, out_ref):
    keys = total_of([keep_ref[...], got_ref[...]]).astype(bf16)
    for y in range(4):
        out_ref[y] = keys


def keys_last_kernel(in_ref, latent_ref, rotary_ref):
    rest = []
    for y in range(4):
        part = in_ref[y].astype(f32)
        latent_ref[y * QUARTER : (y + 1) * QUARTER, :] = part[:, 0:DC]
        rest.append(part[:, DC:WIDE])
    rotary_ref[...] = jnp.concatenate(rest, axis=0).T[0:DR, :]


def fetch(block, slot):
    axes, sizes = ("zl", "c", "zh", "y"), (8, 2, 2, 4)
    pairs = []
    for place in range(16):
        for c in range(2):
            for y in range(4):
                step = FETCH[c][y][slot]
                if step is not None:
                    ends = []
                    for z in ((place + step) % 16, place):
                        ends.append((((z % 8) * 2 + c) * 2 + z // 8) * 4 + y)
                    pairs.append(tuple(ends))
    return lax.ppermute(block, axes, pairs)


def across(block, axis, step):
    n = lax.axis_size(axis)
    return lax.ppermute(block, axis, [(i, i ^ step) for i in range(n)])


def over_edge(block):
    def partner(place):
        return (place + (4 if place % 8 >= 4 else -4)) % 16

    def index(place):
        return place % 8 * 2 + place // 8

    return lax.ppermute(block, ("zl", "zh"), [(index(p), index(partner(p))) for p in range(16)])


def quads(blocks):
    groups = [[0, 1, 2, 3], [4, 5, 6, 7]]
    return lax.all_to_all(blocks, "zl", 0, 0, tiled=True, axis_index_groups=groups)


def everyone(blocks, axes):
    return lax.all_to_all(blocks, axes, 0, 0, tiled=True)


def shards(nope, rotary, latent, keys, upstream, codes, scale, positions):
    weight_send, pack = call(
        prepare_kernel,
        (shape(RANKS, WROWS, WIDE), shape(TOK, WIDE)),
        (latent, keys.T, codes.reshape(WROWS, DC), scale, positions),
        scratch=(
            pltpu.VMEM((DR, TOK), bf16),
            pltpu.VMEM((WROWS, DC), jnp.int32),
            pltpu.SMEM((2, HEADS), f32),
            pltpu.SMEM((TOK,), jnp.int32),
            pltpu.SemaphoreType.DMA((5,)),
        ),
        hbm=(0, 1, 2, 3, 4),
        name="prepare",
        vmem=56,
    )
    weight_ranks = everyone(weight_send, "zl")
    first, second = fetch(pack, 0), fetch(pack, 1)
    together = lax.optimization_barrier
    weight_ranks, first, second = together((weight_ranks, first, second))
    (latent_spread,) = call(
        spread_latent_kernel, (shape(4, 2 * TOK, WIDE),), (first, second), name="spread_latent"
    )
    latent_all = everyone(latent_spread, "y")
    (w_own,) = call(
        order_weight_kernel, (shape(128, DC),), (weight_ranks.reshape(128, WIDE),), name="order_weight"
    )
    for size, step in ((256, 1), (512, 3)):
        (w_own,) = call(join_kernel, (shape(size, DC),), (w_own, across(w_own, "x", step)), name="join")
    w_other = across(w_own, "c", 1)
    latent_all, w_own, w_other = together((latent_all, w_own, w_other))
    runs = weight_ranks[:, 0, DC : DC + 2].astype(jnp.int32).reshape(16)
    dkey, own, other, dq, weight = call(
        attention_kernel,
        (
            shape(4, 256, WIDE),
            shape(512, DC),
            shape(512, DC),
            shape(1024, WIDE),
            shape(1024, DC),
        ),
        (
            runs,
            positions,
            pack,
            latent_all,
            w_own,
            w_other,
            nope.reshape(1024, DN),
            rotary,
            upstream.reshape(1024, DC),
        ),
        scratch=(
            pltpu.VMEM((1024, WIDE), bf16),
            pltpu.VMEM((1024, WIDE), bf16),
            pltpu.VMEM((4, BLOCK, ROWS), f32),
            pltpu.VMEM((4, BLOCK, ROWS), f32),
            pltpu.VMEM((1024, WIDE), f32),
            pltpu.VMEM((ROWS, WIDE), f32),
            pltpu.VMEM((1024, DN), bf16),
            pltpu.VMEM((1024, DC), bf16),
        ),
        smem=(0, 1),
        flops=2 * 512 * 1280 * 2944,
        name="attention",
        vmem=56,
    )
    nope_grad, rot_grad = call(
        query_grads_kernel,
        (shape(1024, DN), shape(TOK, HEADS * DR)),
        (dq, weight),
        scratch=(pltpu.VMEM((1024, DN), bf16),),
        flops=2 * 1024 * 128 * 768,
        name="query_grads",
    )
    def folded(body, size, ins, name):
        return call(body, (shape(size, DC, dtype=f32), shape(size, DC)), ins, name=name)

    keep, send = folded(master_plane_kernel, 256, (own, across(other, "c", 1)), "master_plane")
    keep, send = folded(fold_kernel, 128, (keep, across(send, "x", 1)), "fold")
    dkey_planes, got = together((everyone(dkey, "y"), across(send, "x", 3)))
    (blocks,) = call(plane_kernel, (shape(4, 96, WIDE),), (dkey_planes, keep, got), name="plane")
    both, keep = call(
        quad_sum_kernel, (shape(80, WIDE), shape(WROWS, DC, dtype=f32)), (quads(blocks),), name="quad_sum"
    )
    got = across(both, "zl", 4)
    keep, send, master_grad = call(
        cross_kernel,
        (shape(QUARTER, WIDE), shape(QUARTER, WIDE), shape(WROWS, DC, dtype=f32)),
        (both, got, keep),
        name="cross",
    )
    (dkey_sum,) = call(
        keys_sum_kernel, (shape(4, QUARTER, WIDE),), (keep, over_edge(send)), name="keys_sum"
    )
    dkey_all = everyone(dkey_sum, "y")
    latent_grad, keys_grad = call(
        keys_last_kernel,
        (shape(TOK, DC, dtype=f32), shape(DR, TOK, dtype=f32)),
        (dkey_all,),
        name="keys_last",
    )
    return (
        nope_grad.reshape(TOK, HEADS, DN),
        rot_grad,
        latent_grad,
        keys_grad.T,
        master_grad.reshape(2, HEADS, DC),
    )


def solution(mesh):
    fine = Mesh(mesh.devices.reshape(8, 4, 2, 2, 4), AXES)
    in_specs = (
        P(SEQ, HEAD, None),
        P(SEQ, HEAD),
        P(SEQ, None),
        P(SEQ, None),
        P(SEQ, HEAD, None),
        P(SEQ, HEAD, None),
        P(SEQ, HEAD),
        P(SEQ),
    )
    out_specs = (
        P(SEQ, HEAD, None),
        P(SEQ, HEAD),
        P(SEQ, None),
        P(SEQ, None),
        P(SEQ, HEAD, None),
    )
    return jax.shard_map(shards, mesh=fine, in_specs=in_specs, out_specs=out_specs, check_vma=False)
```

```python
import math

import jax
import jax.numpy as jnp
from jax import lax
from jax.experimental import pallas as pl
from jax.experimental.pallas import tpu as pltpu
from jax.sharding import Mesh, PartitionSpec as P

RANKS = 8
HEADS = 8
HALF = 64
TOK = 128
DN = 128
DC = 512
DR = 64
WIDE = 640
BLOCK = 256
ROWS = HALF * HEADS
QUARTER = 32
WROWS = 16
FACTOR = 1.0 / math.sqrt(DN + DR)
LOG2E = 1.0 / math.log(2.0)
MASKED = -1e30
MIB = 1024 * 1024

bf16 = jnp.bfloat16
f32 = jnp.float32

AXES = ("zl", "x", "c", "zh", "y")
SEQ = ("zl", "x", "c")
HEAD = ("zh", "y")


def nn(a, b):
    return lax.dot_general(a, b, (((1,), (0,)), ((), ())), preferred_element_type=f32)


def nt(a, b):
    return lax.dot_general(a, b, (((1,), (1,)), ((), ())), preferred_element_type=f32)


def tn(a, b):
    return lax.dot_general(a, b, (((0,), (0,)), ((), ())), preferred_element_type=f32)


def iota(shape, axis):
    return lax.broadcasted_iota(jnp.int32, shape, axis)


def chosen(condition):
    return jnp.where(condition, 1.0, 0.0).astype(bf16)


def head_major():
    out, inp = iota((128, 128), 0), iota((128, 128), 1)
    return chosen(inp == (out % 16) * 8 + out // 16)


def token_major():
    out, inp = iota((128, 128), 0), iota((128, 128), 1)
    return chosen(inp == (out % 8) * 16 + out // 8)


def weight_order(row):
    x, c = lax.axis_index("x"), lax.axis_index("c")
    core, step, rank, n = c ^ (row // 64), (row // 16) % 4, (row % 16) // 2, row % 2
    return rank * 16 + (x ^ step) * 4 + core * 2 + n


FETCH = (((1, -3), (-1, 3), (2, -2), (4, None)), ((-1, 3), (1, -3), (2, -2), (-4, None)))


def call(body, outs, ins, scratch=(), flops=0, smem=(), hbm=(), name=None, vmem=6, out_any=False):
    nbytes = sum(math.prod(s.shape) * s.dtype.itemsize for s in list(outs) + list(ins))
    spaces = [
        pltpu.SMEM if i in smem else pl.ANY if i in hbm else pltpu.VMEM for i in range(len(ins))
    ]
    specs = [pl.BlockSpec(memory_space=space) for space in spaces]
    return pl.pallas_call(
        body,
        out_shape=outs,
        in_specs=specs,
        out_specs=[pl.BlockSpec(memory_space=pl.ANY if out_any else pltpu.VMEM) for _ in outs],
        scratch_shapes=list(scratch),
        compiler_params=pltpu.CompilerParams(vmem_limit_bytes=vmem * MIB),
        cost_estimate=pl.CostEstimate(flops=flops, bytes_accessed=nbytes, transcendentals=0),
        name=name,
    )(*ins)


def shape(*dims, dtype=bf16):
    return jax.ShapeDtypeStruct(dims, dtype)


def prepare_kernel(
    lat_hbm,
    rot_hbm,
    codes_hbm,
    scale_hbm,
    pos_hbm,
    weight_out,
    pack_out,
    rot_ref,
    codes_ref,
    scale_ref,
    pos_ref,
    sems,
):
    pairs = (
        (codes_hbm, codes_ref),
        (scale_hbm, scale_ref),
        (pos_hbm, pos_ref),
        (rot_hbm, rot_ref),
        (lat_hbm, pack_out.at[:, 0:DC]),
    )
    copies = [pltpu.make_async_copy(src, dst, sems.at[i]) for i, (src, dst) in enumerate(pairs)]
    for copy in copies:
        copy.start()
    for copy in copies:
        copy.wait()
    codes = codes_ref[...]
    levels = codes + (16 * (codes >> 4) + 8) + (64 * (codes >> 6) + 32)
    row = iota((WROWS, DC), 0)
    scale = jnp.zeros((WROWS, DC), f32)
    for i in range(WROWS):
        scale = jnp.where(row == i, scale_ref[i // HEADS, i % HEADS], scale)
    weight = (scale * levels.astype(f32) / 3.0).astype(bf16)
    lane = iota((WROWS, 128), 1)
    run = [(pos_ref[half * HALF] >> 6).astype(f32) for half in range(2)]
    rest = jnp.where(lane == 0, run[0], jnp.where(lane == 1, run[1], 0.0)).astype(bf16)
    for r in range(RANKS):
        weight_out[r, :, 0:DC] = weight
        weight_out[r, :, DC:WIDE] = rest
    widen = chosen(iota((DR, 128), 0) == iota((DR, 128), 1))
    pack_out[:, DC:WIDE] = tn(rot_ref[...], widen).astype(bf16)


def order_weight_kernel(in_ref, out_ref):
    out, inp = iota((128, 128), 0), iota((128, 128), 1)
    head, rank, n = out // 16, (out % 16) // 2, out % 2
    out_ref[...] = nn(chosen(inp == rank * 16 + n * 8 + head), in_ref[:, 0:DC]).astype(bf16)


def join_kernel(*refs):
    size = refs[0].shape[0]
    for i, part in enumerate(refs[:-1]):
        refs[-1][i * size : (i + 1) * size, :] = part[...]


def spread_latent_kernel(first, second, out_ref):
    for y in range(4):
        out_ref[y, 0:TOK, :] = first[...]
        out_ref[y, TOK : 2 * TOK, :] = second[...]


def order_queries(nope_ref, rot_ref, nope_out, query):
    by_head = head_major()
    inp, out = iota((DN, DN), 0), iota((DN, DN), 1)
    reorder = chosen(inp == weight_order(out))
    for g in range(TOK // 16):
        half, start = g // 4, (g % 4) * 16
        rows = slice(g * 128, (g + 1) * 128)
        nope = nn(nn(by_head, nope_ref[rows, :]).astype(bf16), reorder).astype(bf16)
        for h in range(HEADS):
            place = (half * HEADS + h) * HALF + start
            nope_out[place : place + 16, :] = nope[h * 16 : (h + 1) * 16, :]
    for h in range(HEADS):
        pick = chosen((inp == out + DR * (h % 2)) & (out < DR))
        turned = nn(rot_ref[:, (h // 2) * 128 : (h // 2 + 1) * 128], pick).astype(bf16)
        for half in range(2):
            place = (half * HEADS + h) * HALF
            query[place : place + HALF, DC:WIDE] = turned[half * HALF : (half + 1) * HALF, :]


def order_upstream(up_ref, up_out):
    by_head = head_major()
    for g in range(TOK // 16):
        half, start = g // 4, (g % 4) * 16
        up = nn(by_head, up_ref[g * 128 : (g + 1) * 128, :]).astype(bf16)
        for h in range(HEADS):
            place = (half * HEADS + h) * HALF + start
            up_out[place : place + 16, :] = up[h * 16 : (h + 1) * 16, :]


def attention_kernel(
    runs_ref,
    pack_any,
    lat_any,
    own_any,
    other_any,
    nope_any,
    rot_any,
    up_any,
    dkey_any,
    master_own_any,
    master_other_any,
    dq_any,
    weight_any,
    keys,
    query,
    score,
    slope,
    dkey,
    dquery,
    nope_in,
    rot_in,
    up_in,
    nope_ref,
    up_ref,
    weight_ref,
    dq_ref,
    dkey_out,
    own_out,
    other_out,
    query_sems,
    key_sems,
    weight_sems,
    out_sems,
):
    zl, c = lax.axis_index("zl"), lax.axis_index("c")

    def place_of(run, start, size):
        return pl.ds(pl.multiple_of(run * HALF + start, size), size)

    def started(pairs, sems, base=0):
        copies = [
            pltpu.make_async_copy(src, dst, sems.at[base + i]) for i, (src, dst) in enumerate(pairs)
        ]
        for copy in copies:
            copy.start()
        return copies

    def finish(copies):
        for copy in copies:
            copy.wait()

    query_copies = started(((nope_any, nope_in), (rot_any, rot_in)), query_sems)
    pairs = []
    for core, part in enumerate((own_any, other_any)):
        for step in range(4):
            at = pl.ds(core * 64 + step * 16, 16)
            pairs.append((part.at[step], weight_ref.at[:, at, :]))
    weight_copies = started(pairs, weight_sems)
    pairs = []
    for half in range(2):
        at = place_of(runs_ref[zl * 2 + half], 0, HALF)
        pairs.append((pack_any.at[pl.ds(half * HALF, HALF), :], keys.at[at, :]))
    for y in range(4):
        for slot in range(2):
            steps = [FETCH[core][y][slot] for core in range(2)]
            if steps[0] is None:
                continue
            rank = (zl + RANKS + jnp.where(c == 0, steps[0], steps[1])) % RANKS
            for half in range(2):
                at = place_of(runs_ref[rank * 2 + half], 0, HALF)
                rows = pl.ds(slot * TOK + half * HALF, HALF)
                pairs.append((lat_any.at[y, rows, :], keys.at[at, :]))
    key_copies = started(pairs, key_sems)
    up_copies = started(((up_any, up_in),), query_sems, 2)
    dkey[...] = jnp.zeros_like(dkey)
    dquery[...] = jnp.zeros_like(dquery)
    finish(query_copies)
    order_queries(nope_in, rot_in, nope_ref, query)
    finish(weight_copies)
    outputs = started([(weight_ref, weight_any)], out_sems)
    for h in range(HEADS):
        pair = [nope_ref[(half * HEADS + h) * HALF : (half * HEADS + h + 1) * HALF, :] for half in range(2)]
        absorbed = nn(jnp.concatenate(pair, axis=0), weight_ref[h])
        for half in range(2):
            at = (half * HEADS + h) * HALF
            query[at : at + HALF, 0:DC] = absorbed[half * HALF : (half + 1) * HALF, :].astype(bf16)
    finish(key_copies)

    own_runs = [runs_ref[zl * 2 + half] for half in range(2)]
    first_count = own_runs[0] // 4 + 1
    steps = []
    for t in range(5):
        second = t >= first_count
        j = jnp.where(second, t - first_count, t)
        half = jnp.where(second, 1, 0)
        steps.append(
            (
                second,
                jnp.where(second, own_runs[1], own_runs[0]),
                j,
                pl.ds(pl.multiple_of(j * BLOCK, BLOCK), BLOCK),
                pl.ds(pl.multiple_of(half * ROWS, ROWS), ROWS),
            )
        )

    def per_half(values, empty, join):
        totals = [jnp.full((1, ROWS), empty, f32) for _ in range(2)]
        for (second, *_), value in zip(steps, values):
            totals[0] = join(totals[0], jnp.where(second, empty, value))
            totals[1] = join(totals[1], jnp.where(second, value, empty))
        return totals

    tops = []
    for t, (second, run, j, at, rows) in enumerate(steps):
        s = nt(keys[at, :], query[rows, :]) * (FACTOR * LOG2E)
        place = run * HALF + iota((1, ROWS), 1) % HALF
        s = jnp.where(j * BLOCK + iota((BLOCK, ROWS), 0) <= place, s, MASKED)
        score[t] = s
        tops.append(jnp.max(s, axis=0, keepdims=True))
    top = per_half(tops, MASKED, jnp.maximum)
    finish(up_copies)
    order_upstream(up_in, up_ref)
    sums, weighted = [], []
    for t, (second, run, j, at, rows) in enumerate(steps):
        d = nt(keys[at, 0:DC], up_ref[rows, :])
        e = jnp.exp2(score[t] - jnp.where(second, top[1], top[0]))
        slope[t] = d
        score[t] = e
        sums.append(jnp.sum(e, axis=0, keepdims=True))
        weighted.append(jnp.sum(e * d, axis=0, keepdims=True))
    inverse = [1.0 / total for total in per_half(sums, 0.0, jnp.add)]
    inner = [w * i for w, i in zip(per_half(weighted, 0.0, jnp.add), inverse)]
    for t, (second, run, j, at, rows) in enumerate(steps):
        prob = score[t] * jnp.where(second, inverse[1], inverse[0])
        grad = (prob * (slope[t] - jnp.where(second, inner[1], inner[0])) * FACTOR).astype(bf16)
        dquery[rows, :] += tn(grad, keys[at, :])
        dkey[at, :] += nn(grad, query[rows, :])
        dkey[at, 0:DC] += nn(prob.astype(bf16), up_ref[rows, :])
    for half in range(2):
        rows = pl.ds(half * ROWS, ROWS)
        dq_ref[rows, :] = dquery[rows, :].astype(bf16)
        outputs += started([(dq_ref.at[rows, :], dq_any.at[rows, :])], out_sems, 1 + half)

    for quarter in range(4):
        for k in range(RANKS):
            run = runs_ref[((zl & 4) ^ k) * 2 + quarter // 2]
            at = place_of(run, (quarter % 2) * QUARTER, QUARTER)
            dkey_out[quarter, k * QUARTER : (k + 1) * QUARTER, :] = dkey[at, :].astype(bf16)
        outputs += started(
            [(dkey_out.at[quarter], dkey_any.at[quarter])], out_sems, 3 + quarter
        )
    for h in range(HEADS):
        places = [slice((half * HEADS + h) * HALF, (half * HEADS + h + 1) * HALF) for half in range(2)]
        nope = jnp.concatenate([nope_ref[p, :] for p in places], axis=0)
        dq = jnp.concatenate([dq_ref[p, 0:DC] for p in places], axis=0)
        master = tn(nope, dq).astype(bf16)
        for core, part in enumerate((own_out, other_out)):
            for step in range(4):
                at = core * 64 + step * 16
                part[step * 128 + h * 16 : step * 128 + h * 16 + 16, :] = master[at : at + 16, :]
    pairs = ((own_out, master_own_any), (other_out, master_other_any))
    outputs += started(pairs, out_sems, 7)
    finish(outputs)


def query_grads_kernel(dq_ref, weight_ref, nope_out, rot_out, scratch):
    out, inp = iota((DN, DN), 1), iota((DN, DN), 0)
    reorder = chosen(out == weight_order(inp))
    i, j = iota((128, 128), 0), iota((128, 128), 1)
    left = chosen((i == j) & (j < DR))
    right = chosen((i == j - DR) & (i < DR))
    for h in range(HEADS):
        places = [slice((half * HEADS + h) * HALF, (half * HEADS + h + 1) * HALF) for half in range(2)]
        dq = jnp.concatenate([dq_ref[p, 0:DC] for p in places], axis=0)
        grad = nt(dq, weight_ref[h]).astype(bf16)
        scratch[h * TOK : (h + 1) * TOK, :] = nn(grad, reorder).astype(bf16)
    by_token = token_major()
    for g in range(TOK // 16):
        rows = [scratch[h * TOK + g * 16 : h * TOK + g * 16 + 16, :] for h in range(HEADS)]
        nope_out[g * 128 : (g + 1) * 128, :] = nn(by_token, jnp.concatenate(rows, axis=0)).astype(bf16)
    for p in range(HEADS // 2):
        sides = []
        for h in (2 * p, 2 * p + 1):
            places = [slice((half * HEADS + h) * HALF, (half * HEADS + h + 1) * HALF) for half in range(2)]
            sides.append(jnp.concatenate([dq_ref[q, DC:WIDE] for q in places], axis=0))
        rot_out[:, p * 128 : (p + 1) * 128] = (nn(sides[0], left) + nn(sides[1], right)).astype(bf16)


def total_of(parts):
    total = parts[0].astype(f32)
    for part in parts[1:]:
        total = total + part.astype(f32)
    return total


def master_plane_kernel(own_ref, got_ref, keep_ref, *sends):
    total = own_ref[...].astype(f32) + got_ref[...].astype(f32)
    keep_ref[...] = total[0:128, :]
    for i, send in enumerate(sends):
        send[...] = total[(i + 1) * 128 : (i + 2) * 128, :].astype(bf16)


def plane_kernel(dkey_ref, keep_ref, *refs):
    keys = total_of([dkey_ref[y] for y in range(4)]).astype(bf16)
    out_ref = refs[-1]
    master = (keep_ref[...] + total_of([part[...] for part in refs[:-1]])).astype(bf16)
    zl = lax.axis_index("zl")
    out, inp = iota((128, 128), 0), iota((128, 128), 1)
    rank, n, head = (out // 16) ^ (zl & 4), (out % 16) // 8, out % 8
    master = nn(chosen(inp == head * 16 + rank * 2 + n), master).astype(bf16)
    blank = jnp.zeros((2 * WROWS, 128), bf16)
    for j in range(4):
        for pair in range(2):
            k = pair * 4 + j
            out_ref[j, pair * QUARTER : (pair + 1) * QUARTER, :] = keys[k * QUARTER : (k + 1) * QUARTER, :]
            at = 2 * QUARTER + pair * WROWS
            out_ref[j, at : at + WROWS, 0:DC] = master[k * WROWS : (k + 1) * WROWS, :]
        out_ref[j, 2 * QUARTER :, DC:WIDE] = blank


def quad_sum_kernel(in_ref, both_out, keep_out):
    total = total_of([in_ref[j] for j in range(4)])
    both_out[0 : 2 * QUARTER, :] = total[0 : 2 * QUARTER, :].astype(bf16)
    both_out[2 * QUARTER :, :] = total[2 * QUARTER + WROWS :, :].astype(bf16)
    keep_out[...] = total[2 * QUARTER : 2 * QUARTER + WROWS, 0:DC]


def cross_kernel(both_ref, got_ref, keep_out, send_out):
    low, high = slice(0, QUARTER), slice(QUARTER, 2 * QUARTER)
    keep_out[...] = total_of([both_ref[low, :], got_ref[high, :]]).astype(bf16)
    send_out[low, :] = total_of([both_ref[high, :], got_ref[low, :]]).astype(bf16)
    send_out[QUARTER:, :] = both_ref[2 * QUARTER :, :]


def keys_sum_kernel(keep_ref, got_ref, master_ref, first_ref, out_ref, master_out):
    keys = total_of([keep_ref[...], got_ref[0:QUARTER, :]]).astype(bf16)
    for y in range(4):
        out_ref[y] = keys
    inside = lax.axis_index("c") == 0
    got = jnp.where(inside, first_ref[2 * QUARTER :, 0:DC].astype(f32), got_ref[QUARTER:, 0:DC].astype(f32))
    master_out[...] = master_ref[...] + got


def keys_last_kernel(in_ref, latent_ref, rotary_ref):
    rest = []
    for y in range(4):
        part = in_ref[y].astype(f32)
        latent_ref[y * QUARTER : (y + 1) * QUARTER, :] = part[:, 0:DC]
        rest.append(part[:, DC:WIDE])
    rotary_ref[...] = jnp.concatenate(rest, axis=0).T[0:DR, :]


def fetch(block, slot):
    axes, sizes = ("zl", "c", "zh", "y"), (8, 2, 2, 4)
    pairs = []
    for place in range(16):
        for c in range(2):
            for y in range(4):
                step = FETCH[c][y][slot]
                if step is not None:
                    ends = []
                    for z in ((place + step) % 16, place):
                        ends.append((((z % 8) * 2 + c) * 2 + z // 8) * 4 + y)
                    pairs.append(tuple(ends))
    return lax.ppermute(block, axes, pairs)


def across(block, axis, step):
    n = lax.axis_size(axis)
    return lax.ppermute(block, axis, [(i, i ^ step) for i in range(n)])


def across_half(block, turn):
    def partner(place, c):
        inside = turn == c
        up = (place % 8 < 4) == inside
        return (place + (4 if up else -4)) % 16

    def index(place, c):
        return (place % 8 * 2 + c) * 2 + place // 8

    pairs = [(index(p, c), index(partner(p, c), c)) for p in range(16) for c in range(2)]
    return lax.ppermute(block, ("zl", "c", "zh"), pairs)


def quads(blocks):
    groups = [[0, 1, 2, 3], [4, 5, 6, 7]]
    return lax.all_to_all(blocks, "zl", 0, 0, tiled=True, axis_index_groups=groups)


def everyone(blocks, axes):
    return lax.all_to_all(blocks, axes, 0, 0, tiled=True)


def shards(nope, rotary, latent, keys, upstream, codes, scale, positions):
    weight_send, pack = call(
        prepare_kernel,
        (shape(RANKS, WROWS, WIDE), shape(TOK, WIDE)),
        (latent, keys.T, codes.reshape(WROWS, DC), scale, positions),
        scratch=(
            pltpu.VMEM((DR, TOK), bf16),
            pltpu.VMEM((WROWS, DC), jnp.int32),
            pltpu.SMEM((2, HEADS), f32),
            pltpu.SMEM((TOK,), jnp.int32),
            pltpu.SemaphoreType.DMA((5,)),
        ),
        hbm=(0, 1, 2, 3, 4),
        name="prepare",
        vmem=56,
    )
    weight_ranks = everyone(weight_send, "zl")
    first, second = fetch(pack, 0), fetch(pack, 1)
    together = lax.optimization_barrier
    weight_ranks, first, second = together((weight_ranks, first, second))
    (latent_spread,) = call(
        spread_latent_kernel, (shape(4, 2 * TOK, WIDE),), (first, second), name="spread_latent"
    )
    latent_all = everyone(latent_spread, "y")
    (w_own,) = call(
        order_weight_kernel, (shape(128, DC),), (weight_ranks.reshape(128, WIDE),), name="order_weight"
    )
    far, left, right = [across(w_own, "x", step) for step in (2, 1, 3)]
    (w_own,) = call(join_kernel, (shape(512, DC),), (w_own, left, far, right), name="join")
    w_other = across(w_own, "c", 1)
    latent_all, w_own, w_other = together((latent_all, w_own, w_other))
    runs = weight_ranks[:, 0, DC : DC + 2].astype(jnp.int32).reshape(16)
    dkey, own, other, dq, weight = call(
        attention_kernel,
        (
            shape(4, 256, WIDE),
            shape(512, DC),
            shape(512, DC),
            shape(1024, WIDE),
            shape(HEADS, DN, DC),
        ),
        (
            runs,
            pack,
            latent_all,
            w_own.reshape(4, HEADS, 16, DC),
            w_other.reshape(4, HEADS, 16, DC),
            nope.reshape(1024, DN),
            rotary,
            upstream.reshape(1024, DC),
        ),
        scratch=(
            pltpu.VMEM((1024, WIDE), bf16),
            pltpu.VMEM((1024, WIDE), bf16),
            pltpu.VMEM((5, BLOCK, ROWS), f32),
            pltpu.VMEM((5, BLOCK, ROWS), f32),
            pltpu.VMEM((1024, WIDE), f32),
            pltpu.VMEM((1024, WIDE), f32),
            pltpu.VMEM((1024, DN), bf16),
            pltpu.VMEM((TOK, HEADS * DR), bf16),
            pltpu.VMEM((1024, DC), bf16),
            pltpu.VMEM((1024, DN), bf16),
            pltpu.VMEM((1024, DC), bf16),
            pltpu.VMEM((HEADS, DN, DC), bf16),
            pltpu.VMEM((1024, WIDE), bf16),
            pltpu.VMEM((4, 256, WIDE), bf16),
            pltpu.VMEM((512, DC), bf16),
            pltpu.VMEM((512, DC), bf16),
            pltpu.SemaphoreType.DMA((3,)),
            pltpu.SemaphoreType.DMA((16,)),
            pltpu.SemaphoreType.DMA((8,)),
            pltpu.SemaphoreType.DMA((9,)),
        ),
        smem=(0,),
        hbm=(1, 2, 3, 4, 5, 6, 7),
        out_any=True,
        flops=2 * 512 * 1280 * 2944,
        name="attention",
        vmem=56,
    )
    keep, left, far, right = call(
        master_plane_kernel,
        (shape(128, DC, dtype=f32),) + (shape(128, DC),) * 3,
        (own, across(other, "c", 1)),
        name="master_plane",
    )
    got = [across(part, "x", step) for part, step in ((far, 2), (left, 1), (right, 3))]
    nope_grad, rot_grad = call(
        query_grads_kernel,
        (shape(1024, DN), shape(TOK, HEADS * DR)),
        (dq, weight),
        scratch=(pltpu.VMEM((1024, DN), bf16),),
        flops=2 * 1024 * 128 * 768,
        name="query_grads",
    )
    dkey_planes, nope_grad, rot_grad, *got = together((everyone(dkey, "y"), nope_grad, rot_grad, *got))
    (blocks,) = call(plane_kernel, (shape(4, 96, WIDE),), (dkey_planes, keep, *got), name="plane")
    both, keep = call(
        quad_sum_kernel, (shape(80, WIDE), shape(WROWS, DC, dtype=f32)), (quads(blocks),), name="quad_sum"
    )
    first = across_half(both, 0)
    own, send = call(
        cross_kernel, (shape(QUARTER, WIDE), shape(QUARTER + WROWS, WIDE)), (both, first), name="cross"
    )
    dkey_sum, master_grad = call(
        keys_sum_kernel,
        (shape(4, QUARTER, WIDE), shape(WROWS, DC, dtype=f32)),
        (own, across_half(send, 1), keep, first),
        name="keys_sum",
    )
    dkey_all = everyone(dkey_sum, "y")
    latent_grad, keys_grad = call(
        keys_last_kernel,
        (shape(TOK, DC, dtype=f32), shape(DR, TOK, dtype=f32)),
        (dkey_all,),
        name="keys_last",
    )
    return (
        nope_grad.reshape(TOK, HEADS, DN),
        rot_grad,
        latent_grad,
        keys_grad.T,
        master_grad.reshape(2, HEADS, DC),
    )


def solution(mesh):
    fine = Mesh(mesh.devices.reshape(8, 4, 2, 2, 4), AXES)
    in_specs = (
        P(SEQ, HEAD, None),
        P(SEQ, HEAD),
        P(SEQ, None),
        P(SEQ, None),
        P(SEQ, HEAD, None),
        P(SEQ, HEAD, None),
        P(SEQ, HEAD),
        P(SEQ),
    )
    out_specs = (
        P(SEQ, HEAD, None),
        P(SEQ, HEAD),
        P(SEQ, None),
        P(SEQ, None),
        P(SEQ, HEAD, None),
    )
    return jax.shard_map(shards, mesh=fine, in_specs=in_specs, out_specs=out_specs, check_vma=False)
```

```python
import math

import jax
import jax.numpy as jnp
from jax import lax
from jax.experimental import pallas as pl
from jax.experimental.pallas import tpu as pltpu
from jax.sharding import Mesh, PartitionSpec as P

RANKS = 8
HEADS = 8
HALF = 64
TOK = 128
DN = 128
DC = 512
DR = 64
WIDE = 640
BLOCK = 256
ROWS = HALF * HEADS
QUARTER = 32
WROWS = 16
FACTOR = 1.0 / math.sqrt(DN + DR)
LOG2E = 1.0 / math.log(2.0)
MASKED = -1e30
MIB = 1024 * 1024

bf16 = jnp.bfloat16
f32 = jnp.float32

AXES = ("zl", "x", "c", "zh", "y")
SEQ = ("zl", "x", "c")
HEAD = ("zh", "y")


def nn(a, b):
    return lax.dot_general(a, b, (((1,), (0,)), ((), ())), preferred_element_type=f32)


def nt(a, b):
    return lax.dot_general(a, b, (((1,), (1,)), ((), ())), preferred_element_type=f32)


def tn(a, b):
    return lax.dot_general(a, b, (((0,), (0,)), ((), ())), preferred_element_type=f32)


def iota(shape, axis):
    return lax.broadcasted_iota(jnp.int32, shape, axis)


def chosen(condition):
    return jnp.where(condition, 1.0, 0.0).astype(bf16)


def head_major():
    out, inp = iota((128, 128), 0), iota((128, 128), 1)
    return chosen(inp == (out % 16) * 8 + out // 16)


def token_major():
    out, inp = iota((128, 128), 0), iota((128, 128), 1)
    return chosen(inp == (out % 8) * 16 + out // 8)


def weight_order(row):
    x, c = lax.axis_index("x"), lax.axis_index("c")
    core, step, rank, n = c ^ (row // 64), (row // 16) % 4, (row % 16) // 2, row % 2
    return rank * 16 + (x ^ step) * 4 + core * 2 + n


FETCH = (((1, -3), (-1, 3), (2, -2), (4, None)), ((-1, 3), (1, -3), (2, -2), (-4, None)))


def call(body, outs, ins, scratch=(), flops=0, smem=(), hbm=(), name=None, vmem=6, out_any=False):
    nbytes = sum(math.prod(s.shape) * s.dtype.itemsize for s in list(outs) + list(ins))
    spaces = [
        pltpu.SMEM if i in smem else pl.ANY if i in hbm else pltpu.VMEM for i in range(len(ins))
    ]
    specs = [pl.BlockSpec(memory_space=space) for space in spaces]
    return pl.pallas_call(
        body,
        out_shape=outs,
        in_specs=specs,
        out_specs=[pl.BlockSpec(memory_space=pl.ANY if out_any else pltpu.VMEM) for _ in outs],
        scratch_shapes=list(scratch),
        compiler_params=pltpu.CompilerParams(vmem_limit_bytes=vmem * MIB),
        cost_estimate=pl.CostEstimate(flops=flops, bytes_accessed=nbytes, transcendentals=0),
        name=name,
    )(*ins)


def shape(*dims, dtype=bf16):
    return jax.ShapeDtypeStruct(dims, dtype)


def prepare_kernel(
    lat_hbm,
    rot_hbm,
    codes_hbm,
    scale_hbm,
    pos_hbm,
    weight_out,
    pack_out,
    rot_ref,
    codes_ref,
    scale_ref,
    pos_ref,
    sems,
):
    pairs = (
        (codes_hbm, codes_ref),
        (scale_hbm, scale_ref),
        (pos_hbm, pos_ref),
        (rot_hbm, rot_ref),
        (lat_hbm, pack_out.at[:, 0:DC]),
    )
    copies = [pltpu.make_async_copy(src, dst, sems.at[i]) for i, (src, dst) in enumerate(pairs)]
    for copy in copies:
        copy.start()
    for copy in copies:
        copy.wait()
    codes = codes_ref[...]
    levels = codes + (16 * (codes >> 4) + 8) + (64 * (codes >> 6) + 32)
    row = iota((WROWS, DC), 0)
    scale = jnp.zeros((WROWS, DC), f32)
    for i in range(WROWS):
        scale = jnp.where(row == i, scale_ref[i // HEADS, i % HEADS], scale)
    weight = (scale * levels.astype(f32) / 3.0).astype(bf16)
    for r in range(RANKS):
        weight_out[r] = weight
    widen = chosen(iota((DR, 128), 0) == iota((DR, 128), 1))
    lane = iota((TOK, 128), 1)
    run = [(pos_ref[half * HALF] >> 6).astype(f32) for half in range(2)]
    rest = tn(rot_ref[...], widen)
    rest = jnp.where(lane == DR, run[0], jnp.where(lane == DR + 1, run[1], rest))
    pack_out[:, DC:WIDE] = rest.astype(bf16)


def order_weight_kernel(in_ref, out_ref):
    out, inp = iota((128, 128), 0), iota((128, 128), 1)
    head, rank, n = out // 16, (out % 16) // 2, out % 2
    out_ref[...] = nn(chosen(inp == rank * 16 + n * 8 + head), in_ref[...]).astype(bf16)


def join_kernel(*refs):
    size = refs[0].shape[0]
    for i, part in enumerate(refs[:-1]):
        refs[-1][i * size : (i + 1) * size, :] = part[...]


def spread_latent_kernel(first, second, out_ref):
    for y in range(4):
        out_ref[y, 0:TOK, :] = first[...]
        out_ref[y, TOK : 2 * TOK, :] = second[...]


def order_queries(nope_ref, rot_ref, nope_out, query):
    by_head = head_major()
    inp, out = iota((DN, DN), 0), iota((DN, DN), 1)
    reorder = chosen(inp == weight_order(out))
    for g in range(TOK // 16):
        half, start = g // 4, (g % 4) * 16
        rows = slice(g * 128, (g + 1) * 128)
        nope = nn(nn(by_head, nope_ref[rows, :]).astype(bf16), reorder).astype(bf16)
        for h in range(HEADS):
            place = (half * HEADS + h) * HALF + start
            nope_out[place : place + 16, :] = nope[h * 16 : (h + 1) * 16, :]
    for h in range(HEADS):
        pick = chosen((inp == out + DR * (h % 2)) & (out < DR))
        turned = nn(rot_ref[:, (h // 2) * 128 : (h // 2 + 1) * 128], pick).astype(bf16)
        for half in range(2):
            place = (half * HEADS + h) * HALF
            query[place : place + HALF, DC:WIDE] = turned[half * HALF : (half + 1) * HALF, :]


def order_upstream(up_ref, up_out):
    by_head = head_major()
    for g in range(TOK // 16):
        half, start = g // 4, (g % 4) * 16
        up = nn(by_head, up_ref[g * 128 : (g + 1) * 128, :]).astype(bf16)
        for h in range(HEADS):
            place = (half * HEADS + h) * HALF + start
            up_out[place : place + 16, :] = up[h * 16 : (h + 1) * 16, :]


def attention_kernel(
    runs_in,
    pos_ref,
    pack_any,
    lat_any,
    own_any,
    other_any,
    nope_any,
    rot_any,
    up_any,
    dkey_any,
    master_own_any,
    master_other_any,
    dq_any,
    weight_any,
    keys,
    query,
    score,
    slope,
    dkey,
    dquery,
    nope_in,
    rot_in,
    up_in,
    nope_ref,
    up_ref,
    weight_ref,
    dq_ref,
    dkey_out,
    own_out,
    other_out,
    query_sems,
    key_sems,
    weight_sems,
    out_sems,
    runs_ref,
):
    zl, c = lax.axis_index("zl"), lax.axis_index("c")

    blocks = []
    for y in range(4):
        for slot in range(2):
            steps = [FETCH[core][y][slot] for core in range(2)]
            if steps[0] is not None:
                rank = (zl + RANKS + jnp.where(c == 0, steps[0], steps[1])) % RANKS
                blocks.append((y, slot, rank))
    for half in range(2):
        runs_ref[zl * 2 + half] = pos_ref[half * HALF] >> 6
        for y, slot, rank in blocks:
            runs_ref[rank * 2 + half] = runs_in[(y * 2 + slot) * 2 + half]

    def place_of(run, start, size):
        return pl.ds(pl.multiple_of(run * HALF + start, size), size)

    def started(pairs, sems, base=0):
        copies = [
            pltpu.make_async_copy(src, dst, sems.at[base + i]) for i, (src, dst) in enumerate(pairs)
        ]
        for copy in copies:
            copy.start()
        return copies

    def finish(copies):
        for copy in copies:
            copy.wait()

    query_copies = started(((nope_any, nope_in), (rot_any, rot_in)), query_sems)
    pairs = []
    for core, part in enumerate((own_any, other_any)):
        for step in range(4):
            at = pl.ds(core * 64 + step * 16, 16)
            pairs.append((part.at[step], weight_ref.at[:, at, :]))
    weight_copies = started(pairs, weight_sems)
    pairs = []
    for half in range(2):
        at = place_of(runs_ref[zl * 2 + half], 0, HALF)
        pairs.append((pack_any.at[pl.ds(half * HALF, HALF), :], keys.at[at, :]))
    for y, slot, rank in blocks:
        for half in range(2):
            at = place_of(runs_ref[rank * 2 + half], 0, HALF)
            rows = pl.ds(slot * TOK + half * HALF, HALF)
            pairs.append((lat_any.at[y, rows, :], keys.at[at, :]))
    key_copies = started(pairs, key_sems)
    up_copies = started(((up_any, up_in),), query_sems, 2)
    dkey[...] = jnp.zeros_like(dkey)
    dquery[...] = jnp.zeros_like(dquery)
    finish(query_copies)
    order_queries(nope_in, rot_in, nope_ref, query)
    finish(weight_copies)
    outputs = started([(weight_ref, weight_any)], out_sems)
    for h in range(HEADS):
        pair = [nope_ref[(half * HEADS + h) * HALF : (half * HEADS + h + 1) * HALF, :] for half in range(2)]
        absorbed = nn(jnp.concatenate(pair, axis=0), weight_ref[h])
        for half in range(2):
            at = (half * HEADS + h) * HALF
            query[at : at + HALF, 0:DC] = absorbed[half * HALF : (half + 1) * HALF, :].astype(bf16)
    finish(key_copies)

    own_runs = [runs_ref[zl * 2 + half] for half in range(2)]
    first_count = own_runs[0] // 4 + 1
    steps = []
    for t in range(5):
        second = t >= first_count
        j = jnp.where(second, t - first_count, t)
        half = jnp.where(second, 1, 0)
        steps.append(
            (
                second,
                jnp.where(second, own_runs[1], own_runs[0]),
                j,
                pl.ds(pl.multiple_of(j * BLOCK, BLOCK), BLOCK),
                pl.ds(pl.multiple_of(half * ROWS, ROWS), ROWS),
            )
        )

    def per_half(values, empty, join):
        totals = [jnp.full((1, ROWS), empty, f32) for _ in range(2)]
        for (second, *_), value in zip(steps, values):
            totals[0] = join(totals[0], jnp.where(second, empty, value))
            totals[1] = join(totals[1], jnp.where(second, value, empty))
        return totals

    tops = []
    for t, (second, run, j, at, rows) in enumerate(steps):
        s = nt(keys[at, :], query[rows, :]) * (FACTOR * LOG2E)
        place = run * HALF + iota((1, ROWS), 1) % HALF
        s = jnp.where(j * BLOCK + iota((BLOCK, ROWS), 0) <= place, s, MASKED)
        score[t] = s
        tops.append(jnp.max(s, axis=0, keepdims=True))
    top = per_half(tops, MASKED, jnp.maximum)
    finish(up_copies)
    order_upstream(up_in, up_ref)
    sums, weighted = [], []
    for t, (second, run, j, at, rows) in enumerate(steps):
        d = nt(keys[at, 0:DC], up_ref[rows, :])
        e = jnp.exp2(score[t] - jnp.where(second, top[1], top[0]))
        slope[t] = d
        score[t] = e
        sums.append(jnp.sum(e, axis=0, keepdims=True))
        weighted.append(jnp.sum(e * d, axis=0, keepdims=True))
    inverse = [1.0 / total for total in per_half(sums, 0.0, jnp.add)]
    inner = [w * i for w, i in zip(per_half(weighted, 0.0, jnp.add), inverse)]
    for t, (second, run, j, at, rows) in enumerate(steps):
        prob = score[t] * jnp.where(second, inverse[1], inverse[0])
        grad = (prob * (slope[t] - jnp.where(second, inner[1], inner[0])) * FACTOR).astype(bf16)
        dquery[rows, :] += tn(grad, keys[at, :])
        dkey[at, :] += nn(grad, query[rows, :])
        dkey[at, 0:DC] += nn(prob.astype(bf16), up_ref[rows, :])
    for half in range(2):
        rows = pl.ds(half * ROWS, ROWS)
        dq_ref[rows, :] = dquery[rows, :].astype(bf16)
        outputs += started([(dq_ref.at[rows, :], dq_any.at[rows, :])], out_sems, 1 + half)

    for quarter in range(4):
        for k in range(RANKS):
            run = runs_ref[((zl & 4) ^ k) * 2 + quarter // 2]
            at = place_of(run, (quarter % 2) * QUARTER, QUARTER)
            dkey_out[quarter, k * QUARTER : (k + 1) * QUARTER, :] = dkey[at, :].astype(bf16)
        outputs += started(
            [(dkey_out.at[quarter], dkey_any.at[quarter])], out_sems, 3 + quarter
        )
    for h in range(HEADS):
        places = [slice((half * HEADS + h) * HALF, (half * HEADS + h + 1) * HALF) for half in range(2)]
        nope = jnp.concatenate([nope_ref[p, :] for p in places], axis=0)
        dq = jnp.concatenate([dq_ref[p, 0:DC] for p in places], axis=0)
        master = tn(nope, dq).astype(bf16)
        for core, part in enumerate((own_out, other_out)):
            for step in range(4):
                at = core * 64 + step * 16
                part[step * 128 + h * 16 : step * 128 + h * 16 + 16, :] = master[at : at + 16, :]
    pairs = ((own_out, master_own_any), (other_out, master_other_any))
    outputs += started(pairs, out_sems, 7)
    finish(outputs)


def query_grads_kernel(dq_ref, weight_ref, nope_out, rot_out, scratch):
    out, inp = iota((DN, DN), 1), iota((DN, DN), 0)
    reorder = chosen(out == weight_order(inp))
    i, j = iota((128, 128), 0), iota((128, 128), 1)
    left = chosen((i == j) & (j < DR))
    right = chosen((i == j - DR) & (i < DR))
    for h in range(HEADS):
        places = [slice((half * HEADS + h) * HALF, (half * HEADS + h + 1) * HALF) for half in range(2)]
        dq = jnp.concatenate([dq_ref[p, 0:DC] for p in places], axis=0)
        grad = nt(dq, weight_ref[h]).astype(bf16)
        scratch[h * TOK : (h + 1) * TOK, :] = nn(grad, reorder).astype(bf16)
    by_token = token_major()
    for g in range(TOK // 16):
        rows = [scratch[h * TOK + g * 16 : h * TOK + g * 16 + 16, :] for h in range(HEADS)]
        nope_out[g * 128 : (g + 1) * 128, :] = nn(by_token, jnp.concatenate(rows, axis=0)).astype(bf16)
    for p in range(HEADS // 2):
        sides = []
        for h in (2 * p, 2 * p + 1):
            places = [slice((half * HEADS + h) * HALF, (half * HEADS + h + 1) * HALF) for half in range(2)]
            sides.append(jnp.concatenate([dq_ref[q, DC:WIDE] for q in places], axis=0))
        rot_out[:, p * 128 : (p + 1) * 128] = (nn(sides[0], left) + nn(sides[1], right)).astype(bf16)


def total_of(parts):
    total = parts[0].astype(f32)
    for part in parts[1:]:
        total = total + part.astype(f32)
    return total


def master_plane_kernel(own_ref, got_ref, keep_ref, *sends):
    total = own_ref[...].astype(f32) + got_ref[...].astype(f32)
    keep_ref[...] = total[0:128, :]
    for i, send in enumerate(sends):
        send[...] = total[(i + 1) * 128 : (i + 2) * 128, :].astype(bf16)


def plane_kernel(dkey_ref, keep_ref, *refs):
    keys = total_of([dkey_ref[y] for y in range(4)]).astype(bf16)
    out_ref = refs[-1]
    master = (keep_ref[...] + total_of([part[...] for part in refs[:-1]])).astype(bf16)
    zl = lax.axis_index("zl")
    out, inp = iota((128, 128), 0), iota((128, 128), 1)
    rank, n, head = (out // 16) ^ (zl & 4), (out % 16) // 8, out % 8
    master = nn(chosen(inp == head * 16 + rank * 2 + n), master).astype(bf16)
    blank = jnp.zeros((2 * WROWS, 128), bf16)
    for j in range(4):
        for pair in range(2):
            k = pair * 4 + j
            out_ref[j, pair * QUARTER : (pair + 1) * QUARTER, :] = keys[k * QUARTER : (k + 1) * QUARTER, :]
            at = 2 * QUARTER + pair * WROWS
            out_ref[j, at : at + WROWS, 0:DC] = master[k * WROWS : (k + 1) * WROWS, :]
        out_ref[j, 2 * QUARTER :, DC:WIDE] = blank


def quad_sum_kernel(in_ref, both_out, keep_out):
    total = total_of([in_ref[j] for j in range(4)])
    both_out[0 : 2 * QUARTER, :] = total[0 : 2 * QUARTER, :].astype(bf16)
    both_out[2 * QUARTER :, :] = total[2 * QUARTER + WROWS :, :].astype(bf16)
    keep_out[...] = total[2 * QUARTER : 2 * QUARTER + WROWS, 0:DC]


def cross_kernel(both_ref, got_ref, keep_out, send_out):
    low, high = slice(0, QUARTER), slice(QUARTER, 2 * QUARTER)
    keep_out[...] = total_of([both_ref[low, :], got_ref[high, :]]).astype(bf16)
    send_out[low, :] = total_of([both_ref[high, :], got_ref[low, :]]).astype(bf16)
    send_out[QUARTER:, :] = both_ref[2 * QUARTER :, :]


def keys_sum_kernel(keep_ref, got_ref, master_ref, first_ref, out_ref, master_out):
    keys = total_of([keep_ref[...], got_ref[0:QUARTER, :]]).astype(bf16)
    for y in range(4):
        out_ref[y] = keys
    inside = lax.axis_index("c") == 0
    got = jnp.where(inside, first_ref[2 * QUARTER :, 0:DC].astype(f32), got_ref[QUARTER:, 0:DC].astype(f32))
    master_out[...] = master_ref[...] + got


def keys_last_kernel(in_ref, latent_ref, rotary_ref):
    rest = []
    for y in range(4):
        part = in_ref[y].astype(f32)
        latent_ref[y * QUARTER : (y + 1) * QUARTER, :] = part[:, 0:DC]
        rest.append(part[:, DC:WIDE])
    rotary_ref[...] = jnp.concatenate(rest, axis=0).T[0:DR, :]


def fetch(block, slot):
    axes, sizes = ("zl", "c", "zh", "y"), (8, 2, 2, 4)
    pairs = []
    for place in range(16):
        for c in range(2):
            for y in range(4):
                step = FETCH[c][y][slot]
                if step is not None:
                    ends = []
                    for z in ((place + step) % 16, place):
                        ends.append((((z % 8) * 2 + c) * 2 + z // 8) * 4 + y)
                    pairs.append(tuple(ends))
    return lax.ppermute(block, axes, pairs)


def across(block, axis, step):
    n = lax.axis_size(axis)
    return lax.ppermute(block, axis, [(i, i ^ step) for i in range(n)])


def across_half(block, turn):
    def partner(place, c):
        inside = turn == c
        up = (place % 8 < 4) == inside
        return (place + (4 if up else -4)) % 16

    def index(place, c):
        return (place % 8 * 2 + c) * 2 + place // 8

    pairs = [(index(p, c), index(partner(p, c), c)) for p in range(16) for c in range(2)]
    return lax.ppermute(block, ("zl", "c", "zh"), pairs)


def quads(blocks):
    groups = [[0, 1, 2, 3], [4, 5, 6, 7]]
    return lax.all_to_all(blocks, "zl", 0, 0, tiled=True, axis_index_groups=groups)


def everyone(blocks, axes):
    return lax.all_to_all(blocks, axes, 0, 0, tiled=True)


def shards(nope, rotary, latent, keys, upstream, codes, scale, positions):
    weight_send, pack = call(
        prepare_kernel,
        (shape(RANKS, WROWS, DC), shape(TOK, WIDE)),
        (latent, keys.T, codes.reshape(WROWS, DC), scale, positions),
        scratch=(
            pltpu.VMEM((DR, TOK), bf16),
            pltpu.VMEM((WROWS, DC), jnp.int32),
            pltpu.SMEM((2, HEADS), f32),
            pltpu.SMEM((TOK,), jnp.int32),
            pltpu.SemaphoreType.DMA((5,)),
        ),
        hbm=(0, 1, 2, 3, 4),
        name="prepare",
        vmem=56,
    )
    weight_ranks = everyone(weight_send, "zl")
    first, second = fetch(pack, 0), fetch(pack, 1)
    together = lax.optimization_barrier
    (latent_spread,) = call(
        spread_latent_kernel, (shape(4, 2 * TOK, WIDE),), (first, second), name="spread_latent"
    )
    weight_ranks, latent_spread = together((weight_ranks, latent_spread))
    latent_all = everyone(latent_spread, "y")
    (w_own,) = call(
        order_weight_kernel, (shape(128, DC),), (weight_ranks.reshape(128, DC),), name="order_weight"
    )
    far, left, right = [across(w_own, "x", step) for step in (2, 1, 3)]
    (w_own,) = call(join_kernel, (shape(512, DC),), (w_own, left, far, right), name="join")
    w_other = across(w_own, "c", 1)
    latent_all, w_own, w_other = together((latent_all, w_own, w_other))
    runs = latent_all.reshape(8, TOK, WIDE)[:, 0, DC + DR : DC + DR + 2].astype(jnp.int32).reshape(16)
    dkey, own, other, dq, weight = call(
        attention_kernel,
        (
            shape(4, 256, WIDE),
            shape(512, DC),
            shape(512, DC),
            shape(1024, WIDE),
            shape(HEADS, DN, DC),
        ),
        (
            runs,
            positions,
            pack,
            latent_all,
            w_own.reshape(4, HEADS, 16, DC),
            w_other.reshape(4, HEADS, 16, DC),
            nope.reshape(1024, DN),
            rotary,
            upstream.reshape(1024, DC),
        ),
        scratch=(
            pltpu.VMEM((1024, WIDE), bf16),
            pltpu.VMEM((1024, WIDE), bf16),
            pltpu.VMEM((5, BLOCK, ROWS), f32),
            pltpu.VMEM((5, BLOCK, ROWS), f32),
            pltpu.VMEM((1024, WIDE), f32),
            pltpu.VMEM((1024, WIDE), f32),
            pltpu.VMEM((1024, DN), bf16),
            pltpu.VMEM((TOK, HEADS * DR), bf16),
            pltpu.VMEM((1024, DC), bf16),
            pltpu.VMEM((1024, DN), bf16),
            pltpu.VMEM((1024, DC), bf16),
            pltpu.VMEM((HEADS, DN, DC), bf16),
            pltpu.VMEM((1024, WIDE), bf16),
            pltpu.VMEM((4, 256, WIDE), bf16),
            pltpu.VMEM((512, DC), bf16),
            pltpu.VMEM((512, DC), bf16),
            pltpu.SemaphoreType.DMA((3,)),
            pltpu.SemaphoreType.DMA((16,)),
            pltpu.SemaphoreType.DMA((8,)),
            pltpu.SemaphoreType.DMA((9,)),
            pltpu.SMEM((16,), jnp.int32),
        ),
        smem=(0, 1),
        hbm=(2, 3, 4, 5, 6, 7, 8),
        out_any=True,
        flops=2 * 512 * 1280 * 2944,
        name="attention",
        vmem=56,
    )
    keep, left, far, right = call(
        master_plane_kernel,
        (shape(128, DC, dtype=f32),) + (shape(128, DC),) * 3,
        (own, across(other, "c", 1)),
        name="master_plane",
    )
    got = [across(part, "x", step) for part, step in ((far, 2), (left, 1), (right, 3))]
    nope_grad, rot_grad = call(
        query_grads_kernel,
        (shape(1024, DN), shape(TOK, HEADS * DR)),
        (dq, weight),
        scratch=(pltpu.VMEM((1024, DN), bf16),),
        flops=2 * 1024 * 128 * 768,
        name="query_grads",
    )
    dkey_planes, nope_grad, rot_grad, *got = together((everyone(dkey, "y"), nope_grad, rot_grad, *got))
    (blocks,) = call(plane_kernel, (shape(4, 96, WIDE),), (dkey_planes, keep, *got), name="plane")
    both, keep = call(
        quad_sum_kernel, (shape(80, WIDE), shape(WROWS, DC, dtype=f32)), (quads(blocks),), name="quad_sum"
    )
    first = across_half(both, 0)
    own, send = call(
        cross_kernel, (shape(QUARTER, WIDE), shape(QUARTER + WROWS, WIDE)), (both, first), name="cross"
    )
    dkey_sum, master_grad = call(
        keys_sum_kernel,
        (shape(4, QUARTER, WIDE), shape(WROWS, DC, dtype=f32)),
        (own, across_half(send, 1), keep, first),
        name="keys_sum",
    )
    dkey_all = everyone(dkey_sum, "y")
    latent_grad, keys_grad = call(
        keys_last_kernel,
        (shape(TOK, DC, dtype=f32), shape(DR, TOK, dtype=f32)),
        (dkey_all,),
        name="keys_last",
    )
    return (
        nope_grad.reshape(TOK, HEADS, DN),
        rot_grad,
        latent_grad,
        keys_grad.T,
        master_grad.reshape(2, HEADS, DC),
    )


def solution(mesh):
    fine = Mesh(mesh.devices.reshape(8, 4, 2, 2, 4), AXES)
    in_specs = (
        P(SEQ, HEAD, None),
        P(SEQ, HEAD),
        P(SEQ, None),
        P(SEQ, None),
        P(SEQ, HEAD, None),
        P(SEQ, HEAD, None),
        P(SEQ, HEAD),
        P(SEQ),
    )
    out_specs = (
        P(SEQ, HEAD, None),
        P(SEQ, HEAD),
        P(SEQ, None),
        P(SEQ, None),
        P(SEQ, HEAD, None),
    )
    return jax.shard_map(shards, mesh=fine, in_specs=in_specs, out_specs=out_specs, check_vma=False)
```

```python
import math

import jax
import jax.numpy as jnp
from jax import lax
from jax.experimental import pallas as pl
from jax.experimental.pallas import tpu as pltpu
from jax.sharding import Mesh, PartitionSpec as P

RANKS = 8
HEADS = 8
HALF = 64
TOK = 128
DN = 128
DC = 512
DR = 64
WIDE = 640
BLOCK = 256
ROWS = HALF * HEADS
QUARTER = 32
WROWS = 16
FACTOR = 1.0 / math.sqrt(DN + DR)
LOG2E = 1.0 / math.log(2.0)
MASKED = -1e30
MIB = 1024 * 1024

bf16 = jnp.bfloat16
f32 = jnp.float32

AXES = ("zl", "x", "c", "zh", "y")
SEQ = ("zl", "x", "c")
HEAD = ("zh", "y")


def nn(a, b):
    return lax.dot_general(a, b, (((1,), (0,)), ((), ())), preferred_element_type=f32)


def nt(a, b):
    return lax.dot_general(a, b, (((1,), (1,)), ((), ())), preferred_element_type=f32)


def tn(a, b):
    return lax.dot_general(a, b, (((0,), (0,)), ((), ())), preferred_element_type=f32)


def iota(shape, axis):
    return lax.broadcasted_iota(jnp.int32, shape, axis)


def chosen(condition):
    return jnp.where(condition, 1.0, 0.0).astype(bf16)


def head_major():
    out, inp = iota((128, 128), 0), iota((128, 128), 1)
    return chosen(inp == (out % 16) * 8 + out // 16)


def token_major():
    out, inp = iota((128, 128), 0), iota((128, 128), 1)
    return chosen(inp == (out % 8) * 16 + out // 8)


def weight_order(row):
    x, c = lax.axis_index("x"), lax.axis_index("c")
    core, step, rank, n = c ^ (row // 64), (row // 16) % 4, (row % 16) // 2, row % 2
    return rank * 16 + (x ^ step) * 4 + core * 2 + n


FETCH = (((1, -3), (-1, 3), (2, -2), (4, None)), ((-1, 3), (1, -3), (2, -2), (-4, None)))


def call(body, outs, ins, scratch=(), flops=0, smem=(), hbm=(), name=None, vmem=6, out_any=False):
    nbytes = sum(math.prod(s.shape) * s.dtype.itemsize for s in list(outs) + list(ins))
    spaces = [
        pltpu.SMEM if i in smem else pl.ANY if i in hbm else pltpu.VMEM for i in range(len(ins))
    ]
    specs = [pl.BlockSpec(memory_space=space) for space in spaces]
    return pl.pallas_call(
        body,
        out_shape=outs,
        in_specs=specs,
        out_specs=[pl.BlockSpec(memory_space=pl.ANY if out_any else pltpu.VMEM) for _ in outs],
        scratch_shapes=list(scratch),
        compiler_params=pltpu.CompilerParams(vmem_limit_bytes=vmem * MIB),
        cost_estimate=pl.CostEstimate(flops=flops, bytes_accessed=nbytes, transcendentals=0),
        name=name,
    )(*ins)


def shape(*dims, dtype=bf16):
    return jax.ShapeDtypeStruct(dims, dtype)


def prepare_kernel(
    lat_hbm,
    rot_hbm,
    codes_hbm,
    scale_hbm,
    pos_hbm,
    weight_out,
    pack_out,
    rot_ref,
    codes_ref,
    scale_ref,
    pos_ref,
    sems,
):
    pairs = (
        (codes_hbm, codes_ref),
        (scale_hbm, scale_ref),
        (pos_hbm, pos_ref),
        (rot_hbm, rot_ref),
        (lat_hbm, pack_out.at[:, 0:DC]),
    )
    copies = [pltpu.make_async_copy(src, dst, sems.at[i]) for i, (src, dst) in enumerate(pairs)]
    for copy in copies:
        copy.start()
    for copy in copies:
        copy.wait()
    codes = codes_ref[...]
    levels = codes + (16 * (codes >> 4) + 8) + (64 * (codes >> 6) + 32)
    row = iota((WROWS, DC), 0)
    scale = jnp.zeros((WROWS, DC), f32)
    for i in range(WROWS):
        scale = jnp.where(row == i, scale_ref[i // HEADS, i % HEADS], scale)
    weight = (scale * levels.astype(f32) / 3.0).astype(bf16)
    for r in range(RANKS):
        weight_out[r] = weight
    widen = chosen(iota((DR, 128), 0) == iota((DR, 128), 1))
    lane = iota((TOK, 128), 1)
    run = [(pos_ref[half * HALF] >> 6).astype(f32) for half in range(2)]
    rest = tn(rot_ref[...], widen)
    rest = jnp.where(lane == DR, run[0], jnp.where(lane == DR + 1, run[1], rest))
    pack_out[:, DC:WIDE] = rest.astype(bf16)


def order_weight_kernel(in_ref, out_ref):
    out, inp = iota((128, 128), 0), iota((128, 128), 1)
    head, rank, n = out // 16, (out % 16) // 2, out % 2
    out_ref[...] = nn(chosen(inp == rank * 16 + n * 8 + head), in_ref[...]).astype(bf16)


def join_kernel(*refs):
    size = refs[0].shape[0]
    for i, part in enumerate(refs[:-1]):
        refs[-1][i * size : (i + 1) * size, :] = part[...]


def spread_latent_kernel(first, second, out_ref):
    for y in range(4):
        out_ref[y, 0:TOK, :] = first[...]
        out_ref[y, TOK : 2 * TOK, :] = second[...]


def order_queries(nope_ref, rot_ref, nope_out, query):
    by_head = head_major()
    inp, out = iota((DN, DN), 0), iota((DN, DN), 1)
    reorder = chosen(inp == weight_order(out))
    for g in range(TOK // 16):
        half, start = g // 4, (g % 4) * 16
        rows = slice(g * 128, (g + 1) * 128)
        nope = nn(nn(by_head, nope_ref[rows, :]).astype(bf16), reorder).astype(bf16)
        for h in range(HEADS):
            place = (half * HEADS + h) * HALF + start
            nope_out[place : place + 16, :] = nope[h * 16 : (h + 1) * 16, :]
    for h in range(HEADS):
        pick = chosen((inp == out + DR * (h % 2)) & (out < DR))
        turned = nn(rot_ref[:, (h // 2) * 128 : (h // 2 + 1) * 128], pick).astype(bf16)
        for half in range(2):
            place = (half * HEADS + h) * HALF
            query[place : place + HALF, DC:WIDE] = turned[half * HALF : (half + 1) * HALF, :]


def order_upstream(up_ref, up_out):
    by_head = head_major()
    for g in range(TOK // 16):
        half, start = g // 4, (g % 4) * 16
        up = nn(by_head, up_ref[g * 128 : (g + 1) * 128, :]).astype(bf16)
        for h in range(HEADS):
            place = (half * HEADS + h) * HALF + start
            up_out[place : place + 16, :] = up[h * 16 : (h + 1) * 16, :]


def attention_kernel(
    runs_in,
    pos_ref,
    pack_any,
    lat_any,
    own_any,
    other_any,
    nope_any,
    rot_any,
    up_any,
    dkey_any,
    master_own_any,
    master_other_any,
    dq_any,
    weight_any,
    keys,
    query,
    score,
    slope,
    dkey,
    dquery,
    nope_in,
    rot_in,
    up_in,
    nope_ref,
    up_ref,
    weight_ref,
    dq_ref,
    dkey_out,
    own_out,
    other_out,
    query_sems,
    key_sems,
    weight_sems,
    out_sems,
    runs_ref,
):
    zl, c = lax.axis_index("zl"), lax.axis_index("c")

    blocks = []
    for y in range(4):
        for slot in range(2):
            steps = [FETCH[core][y][slot] for core in range(2)]
            if steps[0] is not None:
                rank = (zl + RANKS + jnp.where(c == 0, steps[0], steps[1])) % RANKS
                blocks.append((y, slot, rank))
    for half in range(2):
        runs_ref[zl * 2 + half] = pos_ref[half * HALF] >> 6
        for y, slot, rank in blocks:
            runs_ref[rank * 2 + half] = runs_in[(y * 2 + slot) * 2 + half]

    def place_of(run, start, size):
        return pl.ds(pl.multiple_of(run * HALF + start, size), size)

    def started(pairs, sems, base=0):
        copies = [
            pltpu.make_async_copy(src, dst, sems.at[base + i]) for i, (src, dst) in enumerate(pairs)
        ]
        for copy in copies:
            copy.start()
        return copies

    def finish(copies):
        for copy in copies:
            copy.wait()

    query_copies = started(((nope_any, nope_in), (rot_any, rot_in)), query_sems)
    pairs = []
    for core, part in enumerate((own_any, other_any)):
        for step in range(4):
            at = pl.ds(core * 64 + step * 16, 16)
            pairs.append((part.at[step], weight_ref.at[:, at, :]))
    weight_copies = started(pairs, weight_sems)
    pairs = []
    for half in range(2):
        at = place_of(runs_ref[zl * 2 + half], 0, HALF)
        pairs.append((pack_any.at[pl.ds(half * HALF, HALF), :], keys.at[at, :]))
    for y, slot, rank in blocks:
        for half in range(2):
            at = place_of(runs_ref[rank * 2 + half], 0, HALF)
            rows = pl.ds(slot * TOK + half * HALF, HALF)
            pairs.append((lat_any.at[y, rows, :], keys.at[at, :]))
    key_copies = started(pairs, key_sems)
    up_copies = started(((up_any, up_in),), query_sems, 2)
    dkey[...] = jnp.zeros_like(dkey)
    dquery[...] = jnp.zeros_like(dquery)
    finish(query_copies)
    order_queries(nope_in, rot_in, nope_ref, query)
    finish(weight_copies)
    outputs = started([(weight_ref, weight_any)], out_sems)
    for h in range(HEADS):
        pair = [nope_ref[(half * HEADS + h) * HALF : (half * HEADS + h + 1) * HALF, :] for half in range(2)]
        absorbed = nn(jnp.concatenate(pair, axis=0), weight_ref[h])
        for half in range(2):
            at = (half * HEADS + h) * HALF
            query[at : at + HALF, 0:DC] = absorbed[half * HALF : (half + 1) * HALF, :].astype(bf16)
    finish(key_copies)

    own_runs = [runs_ref[zl * 2 + half] for half in range(2)]
    first_count = own_runs[0] // 4 + 1
    steps = []
    for t in range(5):
        second = t >= first_count
        j = jnp.where(second, t - first_count, t)
        half = jnp.where(second, 1, 0)
        steps.append(
            (
                second,
                jnp.where(second, own_runs[1], own_runs[0]),
                j,
                pl.ds(pl.multiple_of(j * BLOCK, BLOCK), BLOCK),
                pl.ds(pl.multiple_of(half * ROWS, ROWS), ROWS),
            )
        )

    def per_half(values, empty, join):
        totals = [jnp.full((1, ROWS), empty, f32) for _ in range(2)]
        for (second, *_), value in zip(steps, values):
            totals[0] = join(totals[0], jnp.where(second, empty, value))
            totals[1] = join(totals[1], jnp.where(second, value, empty))
        return totals

    tops = []
    for t, (second, run, j, at, rows) in enumerate(steps):
        s = nt(keys[at, :], query[rows, :]) * (FACTOR * LOG2E)
        place = run * HALF + iota((1, ROWS), 1) % HALF
        s = jnp.where(j * BLOCK + iota((BLOCK, ROWS), 0) <= place, s, MASKED)
        score[t] = s
        tops.append(jnp.max(s, axis=0, keepdims=True))
    top = per_half(tops, MASKED, jnp.maximum)
    finish(up_copies)
    order_upstream(up_in, up_ref)
    sums, weighted = [], []
    for t, (second, run, j, at, rows) in enumerate(steps):
        d = nt(keys[at, 0:DC], up_ref[rows, :])
        e = jnp.exp2(score[t] - jnp.where(second, top[1], top[0]))
        slope[t] = d
        score[t] = e
        sums.append(jnp.sum(e, axis=0, keepdims=True))
        weighted.append(jnp.sum(e * d, axis=0, keepdims=True))
    inverse = [1.0 / total for total in per_half(sums, 0.0, jnp.add)]
    inner = [w * i for w, i in zip(per_half(weighted, 0.0, jnp.add), inverse)]
    for t, (second, run, j, at, rows) in enumerate(steps):
        prob = score[t] * jnp.where(second, inverse[1], inverse[0])
        grad = (prob * (slope[t] - jnp.where(second, inner[1], inner[0])) * FACTOR).astype(bf16)
        dquery[rows, :] += tn(grad, keys[at, :])
        dkey[at, :] += nn(grad, query[rows, :])
        dkey[at, 0:DC] += nn(prob.astype(bf16), up_ref[rows, :])
    for half in range(2):
        rows = pl.ds(half * ROWS, ROWS)
        dq_ref[rows, :] = dquery[rows, :].astype(bf16)
        outputs += started([(dq_ref.at[rows, :], dq_any.at[rows, :])], out_sems, 1 + half)

    for quarter in range(4):
        for k in range(RANKS):
            run = runs_ref[((zl & 4) ^ k) * 2 + quarter // 2]
            at = place_of(run, (quarter % 2) * QUARTER, QUARTER)
            dkey_out[quarter, k * QUARTER : (k + 1) * QUARTER, :] = dkey[at, :].astype(bf16)
        outputs += started(
            [(dkey_out.at[quarter], dkey_any.at[quarter])], out_sems, 3 + quarter
        )
    for h in range(HEADS):
        places = [slice((half * HEADS + h) * HALF, (half * HEADS + h + 1) * HALF) for half in range(2)]
        nope = jnp.concatenate([nope_ref[p, :] for p in places], axis=0)
        dq = jnp.concatenate([dq_ref[p, 0:DC] for p in places], axis=0)
        master = tn(nope, dq).astype(bf16)
        for core, part in enumerate((own_out, other_out)):
            for step in range(4):
                at = core * 64 + step * 16
                part[step * 128 + h * 16 : step * 128 + h * 16 + 16, :] = master[at : at + 16, :]
    pairs = ((own_out, master_own_any), (other_out, master_other_any))
    outputs += started(pairs, out_sems, 7)
    finish(outputs)


def query_grads_kernel(dq_ref, weight_ref, nope_out, rot_out, scratch):
    out, inp = iota((DN, DN), 1), iota((DN, DN), 0)
    reorder = chosen(out == weight_order(inp))
    i, j = iota((128, 128), 0), iota((128, 128), 1)
    left = chosen((i == j) & (j < DR))
    right = chosen((i == j - DR) & (i < DR))
    for h in range(HEADS):
        places = [slice((half * HEADS + h) * HALF, (half * HEADS + h + 1) * HALF) for half in range(2)]
        dq = jnp.concatenate([dq_ref[p, 0:DC] for p in places], axis=0)
        grad = nt(dq, weight_ref[h]).astype(bf16)
        scratch[h * TOK : (h + 1) * TOK, :] = nn(grad, reorder).astype(bf16)
    by_token = token_major()
    for g in range(TOK // 16):
        rows = [scratch[h * TOK + g * 16 : h * TOK + g * 16 + 16, :] for h in range(HEADS)]
        nope_out[g * 128 : (g + 1) * 128, :] = nn(by_token, jnp.concatenate(rows, axis=0)).astype(bf16)
    for p in range(HEADS // 2):
        sides = []
        for h in (2 * p, 2 * p + 1):
            places = [slice((half * HEADS + h) * HALF, (half * HEADS + h + 1) * HALF) for half in range(2)]
            sides.append(jnp.concatenate([dq_ref[q, DC:WIDE] for q in places], axis=0))
        rot_out[:, p * 128 : (p + 1) * 128] = (nn(sides[0], left) + nn(sides[1], right)).astype(bf16)


def total_of(parts):
    total = parts[0].astype(f32)
    for part in parts[1:]:
        total = total + part.astype(f32)
    return total


def master_plane_kernel(own_ref, got_ref, keep_ref, *sends):
    total = own_ref[...].astype(f32) + got_ref[...].astype(f32)
    keep_ref[...] = total[0:128, :]
    for i, send in enumerate(sends):
        send[...] = total[(i + 1) * 128 : (i + 2) * 128, :].astype(bf16)


def plane_kernel(dkey_ref, keep_ref, *refs):
    keys = total_of([dkey_ref[y] for y in range(4)]).astype(bf16)
    out_ref = refs[-1]
    master = (keep_ref[...] + total_of([part[...] for part in refs[:-1]])).astype(bf16)
    zl = lax.axis_index("zl")
    out, inp = iota((128, 128), 0), iota((128, 128), 1)
    rank, n, head = (out // 16) ^ (zl & 4), (out % 16) // 8, out % 8
    master = nn(chosen(inp == head * 16 + rank * 2 + n), master).astype(bf16)
    blank = jnp.zeros((2 * WROWS, 128), bf16)
    for j in range(4):
        for pair in range(2):
            k = pair * 4 + j
            out_ref[j, pair * QUARTER : (pair + 1) * QUARTER, :] = keys[k * QUARTER : (k + 1) * QUARTER, :]
            at = 2 * QUARTER + pair * WROWS
            out_ref[j, at : at + WROWS, 0:DC] = master[k * WROWS : (k + 1) * WROWS, :]
        out_ref[j, 2 * QUARTER :, DC:WIDE] = blank


def quad_sum_kernel(in_ref, both_out, keep_out):
    total = total_of([in_ref[j] for j in range(4)])
    both_out[0 : 2 * QUARTER, :] = total[0 : 2 * QUARTER, :].astype(bf16)
    both_out[2 * QUARTER :, :] = total[2 * QUARTER + WROWS :, :].astype(bf16)
    keep_out[...] = total[2 * QUARTER : 2 * QUARTER + WROWS, 0:DC]


def cross_kernel(both_ref, got_ref, keep_out, send_out):
    low, high = slice(0, QUARTER), slice(QUARTER, 2 * QUARTER)
    keep_out[...] = total_of([both_ref[low, :], got_ref[high, :]]).astype(bf16)
    send_out[low, :] = total_of([both_ref[high, :], got_ref[low, :]]).astype(bf16)
    send_out[QUARTER:, :] = both_ref[2 * QUARTER :, :]


def keys_sum_kernel(keep_ref, got_ref, master_ref, first_ref, out_ref, master_out):
    keys = total_of([keep_ref[...], got_ref[0:QUARTER, :]]).astype(bf16)
    for y in range(4):
        out_ref[y] = keys
    inside = lax.axis_index("c") == 0
    got = jnp.where(inside, first_ref[2 * QUARTER :, 0:DC].astype(f32), got_ref[QUARTER:, 0:DC].astype(f32))
    master_out[...] = master_ref[...] + got


def keys_last_kernel(in_ref, latent_ref, rotary_ref):
    rest = []
    for y in range(4):
        part = in_ref[y].astype(f32)
        latent_ref[y * QUARTER : (y + 1) * QUARTER, :] = part[:, 0:DC]
        rest.append(part[:, DC:WIDE])
    rotary_ref[...] = jnp.concatenate(rest, axis=0).T[0:DR, :]


def fetch(block, slot):
    axes, sizes = ("zl", "c", "zh", "y"), (8, 2, 2, 4)
    pairs = []
    for place in range(16):
        for c in range(2):
            for y in range(4):
                step = FETCH[c][y][slot]
                if step is not None:
                    ends = []
                    for z in ((place + step) % 16, place):
                        ends.append((((z % 8) * 2 + c) * 2 + z // 8) * 4 + y)
                    pairs.append(tuple(ends))
    return lax.ppermute(block, axes, pairs)


def across(block, axis, step):
    n = lax.axis_size(axis)
    return lax.ppermute(block, axis, [(i, i ^ step) for i in range(n)])


def across_half(block, turn):
    def partner(place, c):
        inside = turn == c
        up = (place % 8 < 4) == inside
        return (place + (4 if up else -4)) % 16

    def index(place, c):
        return (place % 8 * 2 + c) * 2 + place // 8

    pairs = [(index(p, c), index(partner(p, c), c)) for p in range(16) for c in range(2)]
    return lax.ppermute(block, ("zl", "c", "zh"), pairs)


def quads(blocks):
    groups = [[0, 1, 2, 3], [4, 5, 6, 7]]
    return lax.all_to_all(blocks, "zl", 0, 0, tiled=True, axis_index_groups=groups)


def everyone(blocks, axes):
    return lax.all_to_all(blocks, axes, 0, 0, tiled=True)


def shards(nope, rotary, latent, keys, upstream, codes, scale, positions):
    weight_send, pack = call(
        prepare_kernel,
        (shape(RANKS, WROWS, DC), shape(TOK, WIDE)),
        (latent, keys.T, codes.reshape(WROWS, DC), scale, positions),
        scratch=(
            pltpu.VMEM((DR, TOK), bf16),
            pltpu.VMEM((WROWS, DC), jnp.int32),
            pltpu.SMEM((2, HEADS), f32),
            pltpu.SMEM((TOK,), jnp.int32),
            pltpu.SemaphoreType.DMA((5,)),
        ),
        hbm=(0, 1, 2, 3, 4),
        name="prepare",
        vmem=56,
    )
    weight_ranks = everyone(weight_send, "zl")
    first, second = fetch(pack, 0), fetch(pack, 1)
    together = lax.optimization_barrier
    (latent_spread,) = call(
        spread_latent_kernel, (shape(4, 2 * TOK, WIDE),), (first, second), name="spread_latent"
    )
    weight_ranks, latent_spread = together((weight_ranks, latent_spread))
    latent_all = everyone(latent_spread, "y")
    (w_own,) = call(
        order_weight_kernel, (shape(128, DC),), (weight_ranks.reshape(128, DC),), name="order_weight"
    )
    far, left, right = [across(w_own, "x", step) for step in (2, 1, 3)]
    (w_own,) = call(join_kernel, (shape(512, DC),), (w_own, left, far, right), name="join")
    w_other = across(w_own, "c", 1)
    runs = latent_all.reshape(8, TOK, WIDE)[:, 0, DC + DR : DC + DR + 2].astype(jnp.int32).reshape(16)
    latent_all, w_own, w_other, runs = together((latent_all, w_own, w_other, runs))
    dkey, own, other, dq, weight = call(
        attention_kernel,
        (
            shape(4, 256, WIDE),
            shape(512, DC),
            shape(512, DC),
            shape(1024, WIDE),
            shape(HEADS, DN, DC),
        ),
        (
            runs,
            positions,
            pack,
            latent_all,
            w_own.reshape(4, HEADS, 16, DC),
            w_other.reshape(4, HEADS, 16, DC),
            nope.reshape(1024, DN),
            rotary,
            upstream.reshape(1024, DC),
        ),
        scratch=(
            pltpu.VMEM((1024, WIDE), bf16),
            pltpu.VMEM((1024, WIDE), bf16),
            pltpu.VMEM((5, BLOCK, ROWS), f32),
            pltpu.VMEM((5, BLOCK, ROWS), f32),
            pltpu.VMEM((1024, WIDE), f32),
            pltpu.VMEM((1024, WIDE), f32),
            pltpu.VMEM((1024, DN), bf16),
            pltpu.VMEM((TOK, HEADS * DR), bf16),
            pltpu.VMEM((1024, DC), bf16),
            pltpu.VMEM((1024, DN), bf16),
            pltpu.VMEM((1024, DC), bf16),
            pltpu.VMEM((HEADS, DN, DC), bf16),
            pltpu.VMEM((1024, WIDE), bf16),
            pltpu.VMEM((4, 256, WIDE), bf16),
            pltpu.VMEM((512, DC), bf16),
            pltpu.VMEM((512, DC), bf16),
            pltpu.SemaphoreType.DMA((3,)),
            pltpu.SemaphoreType.DMA((16,)),
            pltpu.SemaphoreType.DMA((8,)),
            pltpu.SemaphoreType.DMA((9,)),
            pltpu.SMEM((16,), jnp.int32),
        ),
        smem=(0, 1),
        hbm=(2, 3, 4, 5, 6, 7, 8),
        out_any=True,
        flops=2 * 512 * 1280 * 2944,
        name="attention",
        vmem=56,
    )
    keep, left, far, right = call(
        master_plane_kernel,
        (shape(128, DC, dtype=f32),) + (shape(128, DC),) * 3,
        (own, across(other, "c", 1)),
        name="master_plane",
    )
    got = [across(part, "x", step) for part, step in ((far, 2), (left, 1), (right, 3))]
    nope_grad, rot_grad = call(
        query_grads_kernel,
        (shape(1024, DN), shape(TOK, HEADS * DR)),
        (dq, weight),
        scratch=(pltpu.VMEM((1024, DN), bf16),),
        flops=2 * 1024 * 128 * 768,
        name="query_grads",
    )
    dkey_planes, nope_grad, rot_grad, *got = together((everyone(dkey, "y"), nope_grad, rot_grad, *got))
    (blocks,) = call(plane_kernel, (shape(4, 96, WIDE),), (dkey_planes, keep, *got), name="plane")
    both, keep = call(
        quad_sum_kernel, (shape(80, WIDE), shape(WROWS, DC, dtype=f32)), (quads(blocks),), name="quad_sum"
    )
    first = across_half(both, 0)
    own, send = call(
        cross_kernel, (shape(QUARTER, WIDE), shape(QUARTER + WROWS, WIDE)), (both, first), name="cross"
    )
    dkey_sum, master_grad = call(
        keys_sum_kernel,
        (shape(4, QUARTER, WIDE), shape(WROWS, DC, dtype=f32)),
        (own, across_half(send, 1), keep, first),
        name="keys_sum",
    )
    dkey_all = everyone(dkey_sum, "y")
    latent_grad, keys_grad = call(
        keys_last_kernel,
        (shape(TOK, DC, dtype=f32), shape(DR, TOK, dtype=f32)),
        (dkey_all,),
        name="keys_last",
    )
    return (
        nope_grad.reshape(TOK, HEADS, DN),
        rot_grad,
        latent_grad,
        keys_grad.T,
        master_grad.reshape(2, HEADS, DC),
    )


def solution(mesh):
    fine = Mesh(mesh.devices.reshape(8, 4, 2, 2, 4), AXES)
    in_specs = (
        P(SEQ, HEAD, None),
        P(SEQ, HEAD),
        P(SEQ, None),
        P(SEQ, None),
        P(SEQ, HEAD, None),
        P(SEQ, HEAD, None),
        P(SEQ, HEAD),
        P(SEQ),
    )
    out_specs = (
        P(SEQ, HEAD, None),
        P(SEQ, HEAD),
        P(SEQ, None),
        P(SEQ, None),
        P(SEQ, HEAD, None),
    )
    return jax.shard_map(shards, mesh=fine, in_specs=in_specs, out_specs=out_specs, check_vma=False)
```
